256 devices in a mesh: dp: 16 (over y_lo, z), seq: 16 (over x, y_hi, core).
Axes of the slice: x: 4, y: 4 (y_hi: 2, y_lo: 2; y = y_hi * 2 + y_lo), z: 8, core: 2. Of those that a mesh axis runs over, the one named last changes fastest.
Arguments:
- q_in: bfloat16 [16, 2048, 1024], P('dp', 'seq'), may hold values from -6 to 6
- k_in: bfloat16 [16, 2048, 512], P('dp', 'seq'), may hold values from -6 to 6
- v_in: bfloat16 [16, 2048, 512], P('dp', 'seq'), may hold values from -6 to 6
- q_gain: float32 [128], replicated, may hold values from 0.7 to 5
- k_gain: float32 [128], replicated, may hold values from 0.7 to 5
- seg_ids: int32 [16, 2048], P('dp'), may hold values from 0 to 3, never falling along the last dimension, each value on 1 to 1536 neighbouring positions
- teacher: bfloat16 [16, 7168, 2048], P('dp', 'seq'), may hold values from -6 to 6
- mapping: bfloat16 [7168, 1024], P('seq'), may hold values from -0.0625 to 0.0625
Outputs:
- dq_in: bfloat16 [16, 2048, 1024], P('dp', 'seq')
- dk_in: bfloat16 [16, 2048, 512], P('dp', 'seq')
- dv_in: bfloat16 [16, 2048, 512], P('dp', 'seq')
- q_gain_grad: float32 [128], replicated
- key_gain_gradient: float32 [128], replicated
The draws below stay inside these ranges and needn't reach their ends.
Inputs may be any that keep to these rules, and one draw needn't show every extreme that they name: `seg_ids`: segment numbers never fall along a sequence; each of the 4 documents has 1 to 1536 tokens, one exactly 1536.
All inputs are finite; a program needn't handle non-finite values.
Results may differ from the reference program's by a relative error of at most 0.035.
The reference program's roundings to bfloat16 on the way (of `probs_low`, `d_out` and `d_scores`) count: a program that leaves them out, or rounds other values in their place, can miss the bound.
Values may be sent and summed in bfloat16 or wider, within the bound.
No kernel may reach another device: no remote copies, remote signals or barrier semaphores. Data moves between devices by JAX's collectives and lax.ppermute only.
A program may use at most 64 MiB of HBM per device.

```python
import math
import jax
import jax.numpy as jnp
import numpy as np
from jax import lax

QUERY_HEADS = 8
KEY_VALUE_HEADS = 4
HEAD_WIDTH = 128
DT = 7168
SEGS = 4
TOK_DEV = 128
PACKED_SEQUENCES = 16
PACKED_LENGTH = 2048
QUERY_FEATURES = 1024
DKV = 512
N_SEQ = 16


def drawn_keys(key):
    return jax.random.truncated_normal(key, -6.0, 6.0, (PACKED_SEQUENCES, PACKED_LENGTH, DKV), jnp.float32)


def draw_k_in(key, part):
    keys_out = drawn_keys(key)
    return keys_out.astype(jnp.bfloat16)


def draw_q_in(key, part):
    own_key = jax.random.fold_in(key, 3)
    queries = jax.random.truncated_normal(own_key, -6.0, 6.0, (PACKED_SEQUENCES, PACKED_LENGTH, QUERY_FEATURES), jnp.float32)
    return queries.astype(jnp.bfloat16)


def draw_q_gain(key, part):
    key = jax.random.fold_in(key, 5)
    return jax.random.uniform(key, (HEAD_WIDTH,), jnp.float32, 2.0, 3.0)


def draw_k_gain(key, part):
    key = jax.random.fold_in(key, 7)
    return jax.random.uniform(key, (HEAD_WIDTH,), jnp.float32, 2.0, 3.0)


def with_spikes(entries, stream_key, source, target, shards_of, factor):
    owner, partner = [(jnp.arange(entries.shape[position]) // (entries.shape[position] // shards_of)).reshape([-1 if axis == position else 1 for axis in range(entries.ndim)]) for position in (source, target)]
    chosen = jax.random.permutation(stream_key, shards_of)[partner]
    strong = (owner == chosen) | (owner == (partner + shards_of // 2) % shards_of)
    return jnp.where(strong, factor * entries, entries)


def shard_levels(key, dims, split, smallest, top_value):
    level, own = 1.0, jax.random.fold_in(key, 6)
    for axis_at, shards_of in split:
        draws = jnp.exp(jax.random.uniform(jax.random.fold_in(own, axis_at), (shards_of,), jnp.float32, smallest / len(split), top_value / len(split)))
        level = level * jnp.repeat(draws, dims[axis_at] // shards_of).reshape([-1 if axis == axis_at else 1 for axis in range(len(dims))])
    return level


def split_up(number_of, total, limit, skew):
    loads = [(1 << 20) // math.isqrt(grade ** skew) + 1 for grade in range(2, number_of + 1)]
    spare, holding = total - limit - (number_of - 1), [1] * (number_of - 1)
    while spare > 0:
        movable = [i for i in range(number_of - 1) if holding[i] < limit]
        mass, budget = sum([loads[i] for i in movable]), spare
        for i in movable:
            extra = min(limit - holding[i], max(1, budget * loads[i] // mass), spare)
            holding[i] = holding[i] + extra
            spare = spare - extra
    return np.array([limit] + holding)


def uneven_parts(key, count, total, limit, slope):
    if count == 2:
        one = jax.random.randint(key, (), max(1, total - limit), min(limit, total - 1) + 1)
        return jnp.stack([one, total - one])
    tallies = jnp.asarray(split_up(count, total, limit, slope), jnp.int32)
    pairs = (count - 1) // 2
    giver, taker = tallies[1:1 + 2 * pairs:2], tallies[2:2 + 2 * pairs:2]
    margin = jnp.minimum(giver - 1, limit - taker)
    passed = jax.random.randint(jax.random.fold_in(key, 1), (pairs,), 0, 1 << 20) % (margin + 1)
    tallies = tallies.at[1:1 + 2 * pairs:2].set(giver - passed).at[2:2 + 2 * pairs:2].set(taker + passed)
    return tallies[jax.random.permutation(jax.random.fold_in(key, 2), count)]


def scatter_about(stream_key, shape, scale, reach, cuts=(), kind=jnp.bfloat16):
    values = scale * jax.random.normal(stream_key, shape, jnp.float32)
    if cuts:
        values = values * shard_levels(stream_key, shape, cuts, -0.22, 0.18)
    return jnp.clip(values, -reach, reach).astype(kind)


def gaussian_with(stream_key, shape, scale, limit, cuts, heavy, held_as=jnp.bfloat16):
    drawn = scale * jax.random.normal(stream_key, shape, jnp.float32)
    if cuts:
        drawn = drawn * shard_levels(stream_key, shape, cuts, -0.22, 0.18)
    return jnp.clip(with_spikes(drawn, jax.random.fold_in(stream_key, 3), *heavy), -limit, limit).astype(held_as)


def setup_inputs(seed: int = 0) -> dict:
    arg_keys = jax.random.split(jax.random.key(seed), 9)
    return {
        "q_in": draw_q_in(jax.random.fold_in(arg_keys[8], 71), 0),
        "k_in": draw_k_in(jax.random.fold_in(arg_keys[8], 71), 0),
        "v_in": scatter_about(arg_keys[2], (PACKED_SEQUENCES, PACKED_LENGTH, DKV), 1.0, 6.0, ((0, 16), (1, 16))),
        "q_gain": draw_q_gain(jax.random.fold_in(arg_keys[8], 71), 0),
        "k_gain": draw_k_gain(jax.random.fold_in(arg_keys[8], 71), 0),
        "seg_ids": jax.vmap(lambda own: jnp.searchsorted(jnp.cumsum(uneven_parts(own, SEGS, PACKED_LENGTH, 3 * PACKED_LENGTH // 4, 0)), jnp.arange(PACKED_LENGTH), side="right"))(jax.random.split(arg_keys[5], PACKED_SEQUENCES)).reshape((PACKED_SEQUENCES, PACKED_LENGTH)).astype(jnp.int32),
        "teacher": gaussian_with(arg_keys[6], (PACKED_SEQUENCES, DT, PACKED_LENGTH), 1.0, 6.0, ((0, 16), (1, 16)), (1, 2, 16, 2.0)),
        "mapping": scatter_about(arg_keys[7], (DT, QUERY_FEATURES), DT ** -0.5, 0.0625, ((0, 16),)),
    }


epsilon = 1e-06

def rounded(value_rows):
    return lax.optimization_barrier(value_rows.astype(jnp.bfloat16)).astype(jnp.float32)

def apply_norm_scale(value_rows):
    scale_rows = lax.rsqrt(lax.optimization_barrier(jnp.mean(value_rows * value_rows, axis=-1, keepdims=True)) + epsilon)
    return (value_rows * scale_rows, scale_rows)

def norm_backward(grad_hat, unit, scale_rows, gain):
    grad_unit = grad_hat * gain
    return scale_rows * (grad_unit - unit * lax.optimization_barrier(jnp.mean(grad_unit * unit, axis=-1, keepdims=True)))

def reference(q_in, k_in, v_in, q_gain, k_gain, seg_ids, teacher, mapping):
    heads_per_group = QUERY_HEADS // KEY_VALUE_HEADS
    factor = HEAD_WIDTH ** (-0.5)
    positions = jnp.arange(PACKED_LENGTH, dtype=jnp.int32)
    mapping_blocks = mapping.reshape(N_SEQ, DT // N_SEQ, QUERY_FEATURES)

    def one_doc(inputs):
        query_document, key_document, value_document, seg_doc, teacher_doc = inputs
        teacher_blocks = teacher_doc.reshape(N_SEQ, DT // N_SEQ, PACKED_LENGTH)

        def add_block(total, pair):
            block_part = lax.dot_general(pair[0], pair[1], (((0,), (0,)), ((), ())), preferred_element_type=jnp.float32)
            return (total + rounded(block_part), None)
        target_outputs = lax.scan(add_block, jnp.zeros((PACKED_LENGTH, QUERY_FEATURES), jnp.float32), (teacher_blocks, mapping_blocks))[0]
        allowed = (positions[None, :] <= positions[:, None]) & (seg_doc[None, :] == seg_doc[:, None])
        query_unit_rows, query_norm_scale = apply_norm_scale(query_document.astype(jnp.float32).reshape(PACKED_LENGTH, KEY_VALUE_HEADS, heads_per_group, HEAD_WIDTH))
        key_unit_rows, key_norm_scale = apply_norm_scale(key_document.astype(jnp.float32).reshape(PACKED_LENGTH, KEY_VALUE_HEADS, HEAD_WIDTH))
        q_hat = rounded(query_unit_rows * q_gain)
        k_hat = rounded(key_unit_rows * k_gain)
        value_rows = value_document.astype(jnp.float32).reshape(PACKED_LENGTH, KEY_VALUE_HEADS, HEAD_WIDTH)
        target_row_block = target_outputs.reshape(PACKED_LENGTH, KEY_VALUE_HEADS, heads_per_group, HEAD_WIDTH)

        def one_group(group):
            q_group, k_group, v_group, goal_group = group
            scores = jnp.einsum('tgd,sd->gts', q_group, k_group) * factor
            row_max = lax.optimization_barrier(jnp.max(jnp.where(allowed, scores, -1e+30), axis=-1))
            row_total = lax.optimization_barrier(jnp.sum(jnp.where(allowed, jnp.exp(scores - row_max[..., None]), 0.0), axis=-1))
            log_total = row_max + jnp.log(row_total)
            probs = jnp.where(allowed, jnp.exp(scores - log_total[..., None]), 0.0)
            probs_low = rounded(probs)
            outputs = jnp.einsum('gts,sd->tgd', probs_low, v_group)
            errors = outputs - goal_group
            d_out = rounded(errors)
            row_delta = lax.optimization_barrier(jnp.sum(d_out * outputs, axis=-1)).T
            d_probs = jnp.einsum('tgd,sd->gts', d_out, v_group)
            d_scores = rounded(factor * probs * (d_probs - row_delta[..., None]))
            d_query = jnp.einsum('gts,sd->tgd', d_scores, k_group)
            split_scores = d_scores.reshape(heads_per_group, N_SEQ, TOK_DEV, PACKED_LENGTH)
            split_probs = probs_low.reshape(heads_per_group, N_SEQ, TOK_DEV, PACKED_LENGTH)
            split_query = q_group.reshape(N_SEQ, TOK_DEV, heads_per_group, HEAD_WIDTH)
            split_out = d_out.reshape(N_SEQ, TOK_DEV, heads_per_group, HEAD_WIDTH)
            d_key = lax.optimization_barrier(jnp.sum(rounded(jnp.einsum('gbts,btgd->bsd', split_scores, split_query)), axis=0))
            d_value = lax.optimization_barrier(jnp.sum(rounded(jnp.einsum('gbts,btgd->bsd', split_probs, split_out)), axis=0))
            return (d_query, d_key, d_value)
        d_query, d_key, d_value = lax.map(one_group, (q_hat.transpose(1, 0, 2, 3), k_hat.transpose(1, 0, 2), value_rows.transpose(1, 0, 2), target_row_block.transpose(1, 0, 2, 3)))
        d_query = d_query.transpose(1, 0, 2, 3)
        d_key = d_key.transpose(1, 0, 2)
        d_value = d_value.transpose(1, 0, 2)
        dq_doc = norm_backward(d_query, query_unit_rows, query_norm_scale, q_gain)
        dk_doc = norm_backward(d_key, key_unit_rows, key_norm_scale, k_gain)
        q_part = lax.optimization_barrier(jnp.sum(d_query * query_unit_rows, axis=(0, 1, 2)))
        k_part = lax.optimization_barrier(jnp.sum(d_key * key_unit_rows, axis=(0, 1)))
        return (dq_doc.reshape(PACKED_LENGTH, QUERY_FEATURES).astype(jnp.bfloat16), dk_doc.reshape(PACKED_LENGTH, DKV).astype(jnp.bfloat16), d_value.reshape(PACKED_LENGTH, DKV).astype(jnp.bfloat16), q_part, k_part)
    dq_all, dk_all, dv_all, q_parts, key_pieces_list = lax.map(one_doc, (q_in, k_in, v_in, seg_ids, teacher))
    q_gain_grad = lax.optimization_barrier(jnp.sum(q_parts, axis=0)) * (PACKED_SEQUENCES * PACKED_LENGTH * QUERY_HEADS) ** (-0.5)
    key_gain_gradient = lax.optimization_barrier(jnp.sum(key_pieces_list, axis=0)) * (PACKED_SEQUENCES * PACKED_LENGTH * KEY_VALUE_HEADS) ** (-0.5)
    return (dq_all, dk_all, dv_all, q_gain_grad, key_gain_gradient)
```

```python
import functools
import math

import jax
import jax.numpy as jnp
from jax import lax
from jax.experimental import pallas as pl
from jax.experimental.pallas import tpu as pltpu
from jax.sharding import PartitionSpec as P


EPS = 1e-06
NEG = -1e30
HEAD = 128
BLK = 128
NX = 4
F32 = jnp.float32
BF16 = jnp.bfloat16
NT = (((1,), (1,)), ((), ()))
VMEM_LIMIT = 48 * 1024 * 1024


def index_of(x, y, c):
    return (x % 4) * 4 + (y % 2) * 2 + (c % 2)


def shift(value, dx, dy, dc):
    pairs = []
    for x in range(4):
        for y in range(2):
            for c in range(2):
                pairs.append((index_of(x, y, c), index_of(x + dx, y + dy, c + dc)))
    return lax.ppermute(value, "seq", pairs)


def flip(value, dp_bits, seq_bits):
    size = 256
    pairs = [(i, ((i // 16) ^ dp_bits) * 16 + ((i % 16) ^ seq_bits)) for i in range(size)]
    return lax.ppermute(value, ("dp", "seq"), pairs)


def sum_over_four(value, first, second):
    both = (first[0] ^ second[0], first[1] ^ second[1])
    a, b, c = (flip(value, *bits) for bits in (first, second, both))
    return (value + a) + (b + c)


def call(kernel, outs, coords, *args, scratch=(), specs=None, out_specs=None, grid=None, flops=0, moved=0):
    whole = pl.BlockSpec(memory_space=pltpu.VMEM)
    in_specs = specs if specs is not None else [whole] * len(args)
    out_specs = out_specs if out_specs is not None else [whole] * len(outs)
    return pl.pallas_call(
        kernel,
        out_shape=outs,
        grid_spec=pltpu.PrefetchScalarGridSpec(
            num_scalar_prefetch=1,
            grid=grid if grid is not None else (1,),
            in_specs=in_specs,
            out_specs=out_specs,
            scratch_shapes=list(scratch),
        ),
        compiler_params=pltpu.CompilerParams(vmem_limit_bytes=VMEM_LIMIT),
        cost_estimate=pl.CostEstimate(flops=flops, bytes_accessed=moved, transcendentals=0),
    )(coords, *args)


def sds(shape, dtype=BF16):
    return jax.ShapeDtypeStruct(shape, dtype)


def pack_kernel(at, q_ref, k_ref, v_ref, *outs):
    x = at[0]
    for dx in range(NX):
        to = (x + dx) % NX
        outs[dx][:, 0:256] = q_ref[:, pl.ds(pl.multiple_of(to * 256, 256), 256)]
        outs[dx][:, 256:384] = k_ref[:, pl.ds(pl.multiple_of(to * 128, 128), 128)]
        outs[dx][:, 384:512] = v_ref[:, pl.ds(pl.multiple_of(to * 128, 128), 128)]


def copy_kernel(at, a_ref, b_ref, out_ref):
    out_ref[:, 0:128] = a_ref[...]
    out_ref[:, 128:256] = b_ref[...]


def goal_kernel(is_first, at, map_a, map_b, own_0, own_1, other, *refs):
    outs, turned = refs[:-1], refs[-1]
    x = at[0]
    step = pl.program_id(0)

    @pl.when(step == 0)
    def _():
        for dx in range(NX):
            cols = pl.ds(pl.multiple_of(((x + dx) % NX) * 256, 256), 256)
            turned[dx, :, 0:448] = map_a[:, cols].T
            turned[dx, :, 512:960] = map_b[:, cols].T

    own = jnp.concatenate([own_0[...], own_1[...]], axis=1)
    for dx in range(NX):
        part = jnp.dot(turned[dx, :, 0:448], own, preferred_element_type=F32)
        part += jnp.dot(turned[dx, :, 512:960], other[...], preferred_element_type=F32)
        part = part.astype(BF16)
        if is_first:
            outs[dx][0] = part
        else:
            outs[0][0, dx] = part


def unit_rows(rows):
    scale = lax.rsqrt(jnp.mean(rows * rows, axis=-1, keepdims=True) + EPS)
    return rows * scale, scale


def forward_kernel(
    at, kv_0, kv_y, kv_c, kv_yc, q_0, q_1, q_2, q_3, spans, q_gain, k_gain,
    k_hat, k_turned, v_all, k_unit, q_hat, outputs, log_total, s_ref, v_turned,
):
    x, y, c = at[0], at[1], at[2]
    for part, dy, dc in ((kv_0, 0, 0), (kv_y, 1, 0), (kv_c, 0, 1), (kv_yc, 1, 1)):
        for dx in range(NX):
            block = ((x + NX - dx) % NX) * 4 + ((y + dy) % 2) * 2 + (c + dc) % 2
            rows = pl.ds(pl.multiple_of(block * BLK, BLK), BLK)
            unit, _ = unit_rows(part[dx, :, 0:128].astype(F32))
            hat = (unit * k_gain[...]).astype(BF16)
            k_unit[rows, :] = unit
            k_hat[rows, :] = hat
            k_turned[:, rows] = hat.T
            value = part[dx, :, 128:256]
            v_all[rows, :] = value
            v_turned[:, rows] = value.T
    for dx, part in enumerate((q_0, q_1, q_2, q_3)):
        i = (x + NX - dx) % NX
        for g in range(2):
            unit, _ = unit_rows(part[:, g * 128 : (g + 1) * 128].astype(F32))
            q_hat[i, g * 128 : (g + 1) * 128, :] = (unit * q_gain[...]).astype(BF16)
    factor = HEAD ** (-0.5)
    for i in range(NX):
        start = spans[i : i + 1, :]
        place = spans[4 + i : 5 + i, :]
        top = jnp.full((1, 256), NEG, F32)
        for j in range(2 * (i + 1)):
            rows = slice(256 * j, 256 * (j + 1))
            s = lax.dot_general(k_hat[rows, :], q_hat[i], NT, preferred_element_type=F32) * factor
            at_key = lax.broadcasted_iota(jnp.int32, (256, 256), 0) + 256 * j
            allowed = at_key >= start
            if j >= 2 * i:
                allowed = allowed & (at_key <= place)
            s = jnp.where(allowed, s, NEG)
            s_ref[rows, :] = s
            top = jnp.maximum(top, jnp.max(s, axis=0, keepdims=True))
        total = jnp.zeros((1, 256), F32)
        for j in range(2 * (i + 1)):
            rows = slice(256 * j, 256 * (j + 1))
            total += jnp.sum(jnp.exp(s_ref[rows, :] - top), axis=0, keepdims=True)
        log_row = top + jnp.log(total)
        log_total[i : i + 1, :] = log_row
        result = jnp.zeros((128, 256), F32)
        for j in range(2 * (i + 1)):
            rows = slice(256 * j, 256 * (j + 1))
            probs_low = jnp.exp(s_ref[rows, :] - log_row).astype(BF16)
            result += jnp.dot(v_turned[:, rows], probs_low, preferred_element_type=F32)
        outputs[i] = result


def backward_kernel(
    at, k_hat, k_turned, v_all, k_unit, q_hat, outputs, log_total, goal_a, goal_b,
    q_0, q_1, q_2, q_3, spans, q_gain, dq_0, dq_1, dq_2, dq_3, send_c, keep_c, gains,
    d_key, d_value, q_rows, dq_rows,
):
    x, y, c = at[0], at[1], at[2]
    factor = HEAD ** (-0.5)
    for dx, part in enumerate((q_0, q_1, q_2, q_3)):
        i = (x + NX - dx) % NX
        for g in range(2):
            q_rows[i, g * 128 : (g + 1) * 128, :] = part[:, g * 128 : (g + 1) * 128]
    q_part = jnp.zeros((1, 128), F32)
    for i in reversed(range(NX)):
        start = spans[i : i + 1, :]
        place = spans[4 + i : 5 + i, :]
        log_row = log_total[i : i + 1, :]
        goal = goal_a if i < 2 else goal_b
        lanes = slice(128 * (i % 2), 128 * (i % 2) + 128)
        goal = jnp.concatenate([goal[0:128, lanes], goal[128:256, lanes]], axis=1)
        out = outputs[i]
        d_out = (out - goal).astype(BF16)
        delta = jnp.sum(d_out.astype(F32) * out, axis=0, keepdims=True)
        d_out_rows = d_out.T
        query = q_hat[i]
        d_query = jnp.zeros((128, 256), F32)
        for j in range(2 * (i + 1)):
            rows = slice(256 * j, 256 * (j + 1))
            s = lax.dot_general(k_hat[rows, :], query, NT, preferred_element_type=F32) * factor
            at_key = lax.broadcasted_iota(jnp.int32, (256, 256), 0) + 256 * j
            allowed = at_key >= start
            if j >= 2 * i:
                allowed = allowed & (at_key <= place)
            probs = jnp.exp(jnp.where(allowed, s, NEG) - log_row)
            d_probs = jnp.dot(v_all[rows, :], d_out, preferred_element_type=F32)
            d_scores = (factor * probs * (d_probs - delta)).astype(BF16)
            new_value = jnp.dot(probs.astype(BF16), d_out_rows, preferred_element_type=F32)
            new_key = jnp.dot(d_scores, query, preferred_element_type=F32)
            if i == NX - 1:
                d_value[rows, :] = new_value
                d_key[rows, :] = new_key
            else:
                d_value[rows, :] += new_value
                d_key[rows, :] += new_key
            d_query += jnp.dot(k_turned[:, rows], d_scores, preferred_element_type=F32)
        unit, scale = unit_rows(q_rows[i].astype(F32))
        grad = d_query.T
        q_part += jnp.sum(grad * unit, axis=0, keepdims=True)
        grad_unit = grad * q_gain[...]
        dq = scale * (grad_unit - unit * jnp.mean(grad_unit * unit, axis=-1, keepdims=True))
        dq = dq.astype(BF16)
        dq_rows[i, :, 0:128] = dq[0:128]
        dq_rows[i, :, 128:256] = dq[128:256]
    for dx, out in enumerate((dq_0, dq_1, dq_2, dq_3)):
        out[...] = dq_rows[(x + dx) % NX]
    k_part = jnp.zeros((1, 128), F32)
    for j in range(8):
        rows = slice(256 * j, 256 * (j + 1))
        k_part += jnp.sum(d_key[rows, :] * k_unit[rows, :], axis=0, keepdims=True)
    gains[...] = jnp.concatenate([q_part, k_part, jnp.zeros((6, 128), F32)], axis=0)
    for out, dc in ((keep_c, 0), (send_c, 1)):
        for dy in range(2):
            for i in range(NX):
                block = i * 4 + ((y + dy) % 2) * 2 + (c + dc) % 2
                rows = pl.ds(pl.multiple_of(block * BLK, BLK), BLK)
                out[dy, i, :, 0:128] = d_key[rows, :].astype(BF16)
                out[dy, i, :, 128:256] = d_value[rows, :].astype(BF16)


def key_kernel(at, mine, from_y, kv_0, k_gain, out_0, out_1, out_2, out_3):
    x = at[0]
    for dx, out in enumerate((out_0, out_1, out_2, out_3)):
        i = (x + dx) % NX
        total = mine[i] + from_y[i].astype(F32)
        raw = kv_0[(NX - dx) % NX, :, 0:128].astype(F32)
        unit, scale = unit_rows(raw)
        grad_unit = total[:, 0:128] * k_gain[...]
        dk = scale * (grad_unit - unit * jnp.mean(grad_unit * unit, axis=-1, keepdims=True))
        out[:, 0:128] = dk.astype(BF16)
        out[:, 128:256] = total[:, 128:256].astype(BF16)


def unpack_kernel(at, q_0, q_1, q_2, q_3, kv_0, kv_1, kv_2, kv_3, dq, dk, dv):
    x = at[0]
    for dx, (q, kv) in enumerate(((q_0, kv_0), (q_1, kv_1), (q_2, kv_2), (q_3, kv_3))):
        j = (x + NX - dx) % NX
        dq[:, pl.ds(pl.multiple_of(j * 256, 256), 256)] = q[...]
        dk[:, pl.ds(pl.multiple_of(j * 128, 128), 128)] = kv[:, 0:128]
        dv[:, pl.ds(pl.multiple_of(j * 128, 128), 128)] = kv[:, 128:256]


def on_device(q_in, k_in, v_in, q_gain, k_gain, seg_ids, teacher, mapping):
    place = lax.axis_index("seq")
    x, y, c = place // 4, (place // 2) % 2, place % 2
    at = jnp.stack([x, y, c]).astype(jnp.int32)
    q_gain_row, k_gain_row = q_gain.reshape(1, HEAD), k_gain.reshape(1, HEAD)
    teacher_slab = teacher[0]
    whole = pl.BlockSpec(memory_space=pltpu.VMEM)

    half = [
        pl.BlockSpec(
            (448, 128),
            functools.partial(
                lambda i2, s, at: (0, 4 * (2 * (s // 2) + i2) + 2 * ((at[1] + s) % 2) + 1 - at[2]), i2
            ),
        )
        for i2 in range(2)
    ]
    teacher_out = call(
        copy_kernel, sds((448, 1024)), at, teacher_slab, teacher_slab,
        specs=half, out_specs=pl.BlockSpec((448, 256), lambda s, at: (0, s)), grid=(4,),
        moved=2 * 448 * 1024 * 2,
    )
    packed = call(
        pack_kernel, [sds((BLK, 512))] * NX, at, q_in[0], k_in[0], v_in[0], moved=2 * BLK * 2048 * 2
    )
    mapping_other = shift(mapping, 0, 0, 1)
    teacher_other = shift(teacher_out, 0, 0, 1)
    pieces = [packed[0]] + [shift(packed[dx], dx, 0, 0) for dx in (1, 3, 2)]
    pieces = [pieces[0], pieces[1], pieces[3], pieces[2]]

    def goal_parts(first):
        base = 0 if first else 2
        own = [
            pl.BlockSpec(
                (448, 128),
                functools.partial(
                    lambda i2, s, at: (0, 4 * (base + i2) + 2 * ((at[1] + s) % 2) + at[2]), i2
                ),
            )
            for i2 in range(2)
        ]
        specs = [whole, whole, *own, pl.BlockSpec((448, 256), lambda s, at: (0, base + s))]
        if first:
            outs = [sds((2, 256, 256))] * NX
            out_specs = [pl.BlockSpec((1, 256, 256), lambda s, at: (s, 0, 0))] * NX
        else:
            outs = [sds((2, NX, 256, 256))]
            out_specs = [pl.BlockSpec((1, NX, 256, 256), lambda s, at: (s, 0, 0, 0))]
        return call(
            functools.partial(goal_kernel, first), outs, at,
            mapping, mapping_other, teacher_slab, teacher_slab, teacher_other,
            specs=specs, out_specs=out_specs, grid=(2,), scratch=[pltpu.VMEM((NX, 256, 1024), BF16)],
            flops=2 * 896 * 1024 * 512, moved=4 * 448 * 1024 * 2,
        )

    parts_a = goal_parts(True)
    (parts_b,) = goal_parts(False)

    kv_0 = jnp.stack([piece[:, 256:512] for piece in pieces])
    kv_y = shift(kv_0, 0, 1, 0)
    kv_c = shift(kv_0, 0, 0, 1)
    kv_yc = shift(kv_y, 0, 0, 1)

    from_x = [shift(parts_a[dx], dx, 0, 0) for dx in (1, 3, 2)]
    sum_a = sum((part.astype(F32) for part in from_x), parts_a[0].astype(F32))
    b_y = shift(parts_b[1], 0, 1, 0)
    sum_b = parts_b[0].astype(F32) + b_y.astype(F32)
    a_y = shift(sum_a[1].astype(BF16), 0, 1, 0)
    b_x = [shift(sum_b[dx].astype(BF16), dx, 0, 0) for dx in (1, 3, 2)]
    goal_a = sum_a[0] + a_y.astype(F32)
    goal_b = sum((part.astype(F32) for part in b_x), sum_b[0])

    segs = seg_ids[0]
    own_segs = lax.dynamic_index_in_dim(segs.reshape(4, 4, BLK), place % 4, 1, keepdims=False)
    starts = sum(
        jnp.where(own_segs >= d, jnp.sum((segs == d - 1).astype(jnp.int32)), 0) for d in range(1, 4)
    )
    places = (
        512 * jnp.arange(4, dtype=jnp.int32)[:, None]
        + BLK * (place % 4)
        + jnp.arange(BLK, dtype=jnp.int32)[None, :]
    )
    spans = jnp.concatenate([starts, places], axis=0).astype(jnp.int32)
    spans = jnp.concatenate([spans, spans], axis=1)

    q_specs = [pl.BlockSpec((BLK, 256), lambda s, at: (0, 0))] * NX
    fwd = call(
        forward_kernel,
        [
            sds((2048, HEAD)), sds((HEAD, 2048)), sds((2048, HEAD)), sds((2048, HEAD), F32),
            sds((NX, 256, HEAD)), sds((NX, HEAD, 256), F32), sds((8, 256), F32),
        ],
        at, kv_0, kv_y, kv_c, kv_yc, *pieces, spans, q_gain_row, k_gain_row,
        specs=[whole] * 4 + q_specs + [whole] * 3,
        scratch=[pltpu.VMEM((2048, 256), F32), pltpu.VMEM((HEAD, 2048), BF16)],
        flops=700_000_000, moved=4_000_000,
    )
    k_hat, k_turned, v_all, k_unit, q_hat, outputs, log_total = fwd
    bwd = call(
        backward_kernel,
        [sds((BLK, 256))] * NX + [sds((2, NX, BLK, 256))] * 2 + [sds((8, HEAD), F32)],
        at, k_hat, k_turned, v_all, k_unit, q_hat, outputs, log_total, goal_a, goal_b,
        *pieces, spans, q_gain_row,
        specs=[whole] * 9 + q_specs + [whole] * 2,
        scratch=[
            pltpu.VMEM((2048, HEAD), F32), pltpu.VMEM((2048, HEAD), F32),
            pltpu.VMEM((NX, 256, HEAD), BF16), pltpu.VMEM((NX, BLK, 256), BF16),
        ],
        flops=1_700_000_000, moved=5_000_000,
    )
    dq_parts, send_c, keep_c, gains = bwd[:4], bwd[4], bwd[5], bwd[6]

    from_c = shift(send_c, 0, 0, 1)
    sum_c = keep_c.astype(F32) + from_c.astype(F32)
    from_y = shift(sum_c[1].astype(BF16), 0, 1, 0)
    dq_got = [dq_parts[0]] + [shift(dq_parts[dx], dx, 0, 0) for dx in (1, 2, 3)]

    total = sum_over_four(gains, (1, 0), (2, 0))
    total = sum_over_four(total, (4, 0), (0, 1))
    total = sum_over_four(total, (8, 0), (0, 2))
    total = sum_over_four(total, (0, 4), (0, 8))

    dkv = call(
        key_kernel, [sds((BLK, 256))] * NX, at, sum_c[0], from_y, kv_0, k_gain_row, moved=2_000_000
    )
    dkv_got = [dkv[0]] + [shift(dkv[dx], dx, 0, 0) for dx in (1, 2, 3)]
    dq, dk, dv = call(
        unpack_kernel, [sds((BLK, 1024)), sds((BLK, 512)), sds((BLK, 512))], at, *dq_got, *dkv_got,
        moved=2 * BLK * 2048 * 2,
    )
    q_gain_grad = total[0] * (1.0 / math.sqrt(262144))
    key_gain_gradient = total[1] * (1.0 / math.sqrt(131072))
    return dq[None], dk[None], dv[None], q_gain_grad, key_gain_gradient


def solution(mesh):
    return jax.shard_map(
        on_device,
        mesh=mesh,
        in_specs=(
            P("dp", "seq", None),
            P("dp", "seq", None),
            P("dp", "seq", None),
            P(),
            P(),
            P("dp", None),
            P("dp", "seq", None),
            P("seq", None),
        ),
        out_specs=(P("dp", "seq", None), P("dp", "seq", None), P("dp", "seq", None), P(), P()),
        check_vma=False,
    )
```

```python
import functools
import math

import jax
import jax.numpy as jnp
from jax import lax
from jax.experimental import pallas as pl
from jax.experimental.pallas import tpu as pltpu
from jax.sharding import PartitionSpec as P


EPS = 1e-06
NEG = -1e30
HEAD = 128
ROWS_A = 160
ROWS_B = 256 - ROWS_A
BLK = 128
NX = 4
F32 = jnp.float32
BF16 = jnp.bfloat16
NT = (((1,), (1,)), ((), ()))
VMEM_LIMIT = 48 * 1024 * 1024
VMEM_MOST = 63 * 1024 * 1024


def index_of(x, y, c):
    return (x % 4) * 4 + (y % 2) * 2 + (c % 2)


def shift(value, dx, dy, dc):
    pairs = []
    for x in range(4):
        for y in range(2):
            for c in range(2):
                pairs.append((index_of(x, y, c), index_of(x + dx, y + dy, c + dc)))
    return lax.ppermute(value, "seq", pairs)


def flip(value, dp_bits, seq_bits):
    size = 256
    pairs = [(i, ((i // 16) ^ dp_bits) * 16 + ((i % 16) ^ seq_bits)) for i in range(size)]
    return lax.ppermute(value, ("dp", "seq"), pairs)


def sum_over_four(value, first, second):
    both = (first[0] ^ second[0], first[1] ^ second[1])
    a, b, c = (flip(value, *bits) for bits in (first, second, both))
    return (value + a) + (b + c)


def along_z(value, step):
    pairs = [((i // 8) * 8 + (i + step) % 8, i) for i in range(16)]
    return lax.ppermute(value, "dp", pairs)


def call(kernel, outs, *args, scratch=(), after=(), hbm_in=False, hbm_out=False, limit=VMEM_LIMIT, flops=1):
    vmem, hbm = pl.BlockSpec(memory_space=pltpu.VMEM), pl.BlockSpec(memory_space=pltpu.HBM)
    used = len(args)

    def body(*refs):
        place = lax.axis_index("seq")
        at = (place // 4, (place // 2) % 2, place % 2, lax.axis_index("dp") % 8)
        kernel(at, *refs[:used], *refs[used + len(after) :])

    return pl.pallas_call(
        body,
        out_shape=outs,
        in_specs=[hbm if hbm_in else vmem] * used + [pl.BlockSpec(memory_space=pl.ANY)] * len(after),
        out_specs=[hbm if hbm_out else vmem] * len(outs),
        scratch_shapes=list(scratch),
        compiler_params=pltpu.CompilerParams(vmem_limit_bytes=limit),
        cost_estimate=pl.CostEstimate(flops=flops, bytes_accessed=1, transcendentals=0),
    )(*args, *after)


def sds(shape, dtype=BF16):
    return jax.ShapeDtypeStruct(shape, dtype)


def goal_kernel(
    at, mapping, teacher, q_ref, k_ref, v_ref, a_other, b_other, a_own, b_own, out_0, out_1, out_2, out_3,
    turned, held_map, held, a_held, b_held, packed, sems, out_sems, pack_sems,
):
    x, y, c = at[0], at[1], at[2]
    copies = [pltpu.make_async_copy(mapping, held_map, sems.at[4])]
    for n in range(4):
        lanes = slice(512 * n, 512 * (n + 1))
        copies.append(pltpu.make_async_copy(teacher.at[:, lanes], held.at[:, lanes], sems.at[n]))
    for copy in copies:
        copy.start()
    outs = (out_0, out_1, out_2, out_3)
    pieces = []
    for dx in range(NX):
        to = (x + dx) % NX
        wide = pl.ds(pl.multiple_of(to * 256, 256), 256)
        narrow = pl.ds(pl.multiple_of(to * 128, 128), 128)
        for n, (ref, cols, lanes) in enumerate(
            ((q_ref, wide, slice(0, 256)), (k_ref, narrow, slice(256, 384)), (v_ref, narrow, slice(384, 512)))
        ):
            piece = pltpu.make_async_copy(ref.at[:, cols], packed.at[dx, :, lanes], pack_sems.at[3 * dx + n])
            piece.start()
            pieces.append(piece)
    copies[0].wait()
    for n in range(NX):
        turned[256 * n : 256 * (n + 1), :] = held_map[:, 256 * n : 256 * (n + 1)].T
    for copy in copies[1:] + pieces:
        copy.wait()
    stores = []
    for dx in range(NX):
        copy = pltpu.make_async_copy(packed.at[dx], outs[dx], pack_sems.at[12 + dx])
        copy.start()
        stores.append(copy)
    for core, a_out, b_out in ((1, a_other, b_other), (0, a_own, b_own)):
        for dy in range(2):
            blocks = [4 * i + 2 * ((y + dy) % 2) + (c + core) % 2 for i in range(4)]
            columns = [held[:, pl.ds(pl.multiple_of(block * BLK, BLK), BLK)] for block in blocks]
            columns = jnp.concatenate(columns, axis=1)
            for dx in range(NX):
                rows = pl.ds(pl.multiple_of(((x + dx) % NX) * 256, 256), 256)
                part = jnp.dot(turned[rows, :], columns, preferred_element_type=F32).astype(BF16)
                a_held[core, dx, dy] = part[:ROWS_A]
                b_held[core, dy, dx] = part[ROWS_A:]
            for n, (held_ref, out) in enumerate(
                ((a_held.at[core, :, dy], a_out.at[:, dy]), (b_held.at[core, dy], b_out.at[dy]))
            ):
                copy = pltpu.make_async_copy(held_ref, out, out_sems.at[4 * core + 2 * dy + n])
                copy.start()
                stores.append(copy)
    for copy in stores:
        copy.wait()


def kv_kernel(at, p_0, p_1, p_2, p_3, out):
    for dx, part in enumerate((p_0, p_1, p_2, p_3)):
        out[dx] = part[:, 256:512]


def pair_kernel(at, own, other, out):
    out[0] = own[...]
    out[1] = other[...]


def unit_rows(rows):
    scale = lax.rsqrt(jnp.mean(rows * rows, axis=-1, keepdims=True) + EPS)
    return rows * scale, scale


def forward_kernel(
    at, kv_both, kv_swapped, q_0, q_1, q_2, q_3, segs, q_gain, k_gain,
    k_hat, k_turned, v_all, k_unit, q_hat, outputs, log_total, spans, s_ref, v_turned,
):
    x, y, c = at[0], at[1], at[2]
    before = []
    for d in range(3):
        hits = jnp.sum((segs[...] == d).astype(F32), axis=1, keepdims=True)
        before.append(jnp.sum(hits, axis=0, keepdims=True).astype(jnp.int32))
    lane = lax.broadcasted_iota(jnp.int32, (1, BLK), 1)
    for i in range(NX):
        block = 4 * i + 2 * y + c
        own = segs[pl.ds(block, 1), :]
        first = sum(jnp.where(own > d, before[d], 0) for d in range(3))
        spans[i : i + 1, :] = jnp.concatenate([first, first], axis=1)
        here = block * BLK + lane
        spans[4 + i : 5 + i, :] = jnp.concatenate([here, here], axis=1)
    for part, dy, dc in ((kv_both, 0, 0), (kv_both, 1, 0), (kv_swapped, 0, 1), (kv_swapped, 1, 1)):
        for dx in range(NX):
            block = ((x + NX - dx) % NX) * 4 + ((y + dy) % 2) * 2 + (c + dc) % 2
            rows = pl.ds(pl.multiple_of(block * BLK, BLK), BLK)
            unit, _ = unit_rows(part[dy, dx, :, 0:128].astype(F32))
            hat = (unit * k_gain[...]).astype(BF16)
            k_unit[rows, :] = unit
            k_hat[rows, :] = hat
            k_turned[:, rows] = hat.T
            value = part[dy, dx, :, 128:256]
            v_all[rows, :] = value
            v_turned[:, rows] = value.T
    for dx, part in enumerate((q_0, q_1, q_2, q_3)):
        i = (x + NX - dx) % NX
        for g in range(2):
            unit, _ = unit_rows(part[:, g * 128 : (g + 1) * 128].astype(F32))
            q_hat[i, g * 128 : (g + 1) * 128, :] = (unit * q_gain[...]).astype(BF16)
    factor = HEAD ** (-0.5)
    for i in range(NX):
        start = spans[i : i + 1, :]
        place = spans[4 + i : 5 + i, :]
        top = jnp.full((1, 256), NEG, F32)
        for j in range(2 * (i + 1)):
            rows = slice(256 * j, 256 * (j + 1))
            s = lax.dot_general(k_hat[rows, :], q_hat[i], NT, preferred_element_type=F32) * factor
            at_key = lax.broadcasted_iota(jnp.int32, (256, 256), 0) + 256 * j
            allowed = at_key >= start
            if j >= 2 * i:
                allowed = allowed & (at_key <= place)
            s = jnp.where(allowed, s, NEG)
            s_ref[rows, :] = s
            top = jnp.maximum(top, jnp.max(s, axis=0, keepdims=True))
        total = jnp.zeros((1, 256), F32)
        for j in range(2 * (i + 1)):
            rows = slice(256 * j, 256 * (j + 1))
            total += jnp.sum(jnp.exp(s_ref[rows, :] - top), axis=0, keepdims=True)
        log_row = top + jnp.log(total)
        log_total[i : i + 1, :] = log_row
        result = jnp.zeros((128, 256), F32)
        for j in range(2 * (i + 1)):
            rows = slice(256 * j, 256 * (j + 1))
            probs_low = jnp.exp(s_ref[rows, :] - log_row).astype(BF16)
            result += jnp.dot(v_turned[:, rows], probs_low, preferred_element_type=F32)
        outputs[i] = result


def backward_kernel(
    at, k_hat, k_turned, v_all, k_unit, q_hat, outputs, log_total, goal_a, goal_b,
    q_0, q_1, q_2, q_3, spans, q_gain, dq_0, dq_1, dq_2, dq_3, send_c, keep_c, gains,
    d_key, d_value, q_rows, dq_rows,
):
    x, y, c = at[0], at[1], at[2]
    factor = HEAD ** (-0.5)
    for dx, part in enumerate((q_0, q_1, q_2, q_3)):
        i = (x + NX - dx) % NX
        for g in range(2):
            q_rows[i, g * 128 : (g + 1) * 128, :] = part[:, g * 128 : (g + 1) * 128]
    q_part = jnp.zeros((1, 128), F32)
    for i in reversed(range(NX)):
        start = spans[i : i + 1, :]
        place = spans[4 + i : 5 + i, :]
        log_row = log_total[i : i + 1, :]
        lanes = slice(128 * i, 128 * (i + 1))
        goal = jnp.concatenate([goal_a[:, lanes], goal_b[:, lanes]], axis=0)
        goal = jnp.concatenate([goal[0:128], goal[128:256]], axis=1)
        out = outputs[i]
        d_out = (out - goal).astype(BF16)
        delta = jnp.sum(d_out.astype(F32) * out, axis=0, keepdims=True)
        d_out_rows = d_out.T
        query = q_hat[i]
        d_query = jnp.zeros((128, 256), F32)
        for j in range(2 * (i + 1)):
            rows = slice(256 * j, 256 * (j + 1))
            s = lax.dot_general(k_hat[rows, :], query, NT, preferred_element_type=F32) * factor
            at_key = lax.broadcasted_iota(jnp.int32, (256, 256), 0) + 256 * j
            allowed = at_key >= start
            if j >= 2 * i:
                allowed = allowed & (at_key <= place)
            probs = jnp.exp(jnp.where(allowed, s, NEG) - log_row)
            d_probs = jnp.dot(v_all[rows, :], d_out, preferred_element_type=F32)
            d_scores = (factor * probs * (d_probs - delta)).astype(BF16)
            new_value = jnp.dot(probs.astype(BF16), d_out_rows, preferred_element_type=F32)
            new_key = jnp.dot(d_scores, query, preferred_element_type=F32)
            if i == NX - 1:
                d_value[rows, :] = new_value
                d_key[rows, :] = new_key
            else:
                d_value[rows, :] += new_value
                d_key[rows, :] += new_key
            d_query += jnp.dot(k_turned[:, rows], d_scores, preferred_element_type=F32)
        unit, scale = unit_rows(q_rows[i].astype(F32))
        grad = d_query.T
        q_part += jnp.sum(grad * unit, axis=0, keepdims=True)
        grad_unit = grad * q_gain[...]
        dq = scale * (grad_unit - unit * jnp.mean(grad_unit * unit, axis=-1, keepdims=True))
        dq = dq.astype(BF16)
        dq_rows[i, :, 0:128] = dq[0:128]
        dq_rows[i, :, 128:256] = dq[128:256]
    for dx, out in enumerate((dq_0, dq_1, dq_2, dq_3)):
        out[...] = dq_rows[(x + dx) % NX]
    k_part = jnp.zeros((1, 128), F32)
    for j in range(8):
        rows = slice(256 * j, 256 * (j + 1))
        k_part += jnp.sum(d_key[rows, :] * k_unit[rows, :], axis=0, keepdims=True)
    gains[...] = jnp.concatenate([q_part, k_part, jnp.zeros((6, 128), F32)], axis=0)
    for out, dc in ((keep_c, 0), (send_c, 1)):
        for dy in range(2):
            for i in range(NX):
                block = i * 4 + ((y + dy) % 2) * 2 + (c + dc) % 2
                rows = pl.ds(pl.multiple_of(block * BLK, BLK), BLK)
                out[dy, i, :, 0:128] = d_key[rows, :].astype(BF16)
                out[dy, i, :, 128:256] = d_value[rows, :].astype(BF16)


def key_kernel(at, mine, from_y, kv_0, k_gain, gains, dq_0, dq_1, dq_2, dq_3, out_0, out_1, out_2, out_3):
    x = at[0]
    for dx, (dq, out) in enumerate(((dq_0, out_0), (dq_1, out_1), (dq_2, out_2), (dq_3, out_3))):
        i = (x + dx) % NX
        total = mine[i] + from_y[i].astype(F32)
        raw = kv_0[(NX - dx) % NX, :, 0:128].astype(F32)
        unit, scale = unit_rows(raw)
        grad_unit = total[:, 0:128] * k_gain[...]
        dk = scale * (grad_unit - unit * jnp.mean(grad_unit * unit, axis=-1, keepdims=True))
        out[0:BLK, 0:256] = dq[...]
        out[0:BLK, 256:384] = dk.astype(BF16)
        out[0:BLK, 384:512] = total[:, 128:256].astype(BF16)
        rest = jnp.concatenate([gains[...], jnp.zeros((8, HEAD), F32)], axis=0)
        for term in range(3):
            high = rest.astype(BF16)
            out[BLK:, 128 * term : 128 * (term + 1)] = high
            rest = rest - high.astype(F32)
        out[BLK:, 384:512] = jnp.zeros((16, HEAD), BF16)


def add_kernel(at, a, b, out):
    out[...] = a[...] + b[...]


def gains_kernel(at, p_0, p_1, p_2, p_3, out, held):
    x = at[0]
    for dx, part in enumerate((p_0, p_1, p_2, p_3)):
        terms = [part[BLK:, 128 * t : 128 * (t + 1)].astype(F32) for t in range(3)]
        held[(x + NX - dx) % NX] = (terms[0] + terms[1]) + terms[2]
    total = (held[0] + held[1]) + (held[2] + held[3])
    out[...] = total[0:8]


def total_kernel(at, mine, above, below, q_out, k_out, held):
    z = at[3]
    for part, step in ((mine, 0), (above, 3), (below, 5)):
        for row, more in ((0, 0), (2, 1), (4, 7)):
            held[(z + step + more) % 8] = part[row : row + 2, :]
    total = ((held[0] + held[1]) + (held[2] + held[3])) + ((held[4] + held[5]) + (held[6] + held[7]))
    q_out[...] = total[0:1] * (1.0 / math.sqrt(262144))
    k_out[...] = total[1:2] * (1.0 / math.sqrt(131072))


def unpack_kernel(at, p_0, p_1, p_2, p_3, dq, dk, dv):
    x = at[0]
    for dx, part in enumerate((p_0, p_1, p_2, p_3)):
        j = (x + NX - dx) % NX
        dq[:, pl.ds(pl.multiple_of(j * 256, 256), 256)] = part[0:BLK, 0:256]
        dk[:, pl.ds(pl.multiple_of(j * 128, 128), 128)] = part[0:BLK, 256:384]
        dv[:, pl.ds(pl.multiple_of(j * 128, 128), 128)] = part[0:BLK, 384:512]


def on_device(q_in, k_in, v_in, q_gain, k_gain, seg_ids, teacher, mapping):
    q_gain_row, k_gain_row = q_gain.reshape(1, HEAD), k_gain.reshape(1, HEAD)
    teacher_slab = teacher[0]

    a_shape, b_shape = sds((NX, 2, ROWS_A, 512)), sds((2, NX, ROWS_B, 512))
    a_other, b_other, a_own, b_own, *packed = call(
        goal_kernel, [a_shape, b_shape, a_shape, b_shape] + [sds((BLK, 512))] * NX,
        mapping, teacher_slab, q_in[0], k_in[0], v_in[0],
        hbm_in=True, hbm_out=True, limit=VMEM_MOST, flops=6_000_000_000,
        scratch=[
            pltpu.VMEM((1024, 448), BF16), pltpu.VMEM((448, 1024), BF16), pltpu.VMEM((448, 2048), BF16),
            pltpu.VMEM((2, NX, 2, ROWS_A, 512), BF16), pltpu.VMEM((2, 2, NX, ROWS_B, 512), BF16),
            pltpu.VMEM((NX, BLK, 512), BF16),
            pltpu.SemaphoreType.DMA((5,)), pltpu.SemaphoreType.DMA((8,)), pltpu.SemaphoreType.DMA((16,)),
        ],
    )
    pieces = [packed[0]] + [shift(packed[dx], dx, 0, 0) for dx in (1, 2, 3)]
    b_swapped = shift(b_other, 0, 0, 1)
    a_swapped = shift(a_other, 0, 0, 1)
    b_send = (b_own[1].astype(F32) + b_swapped[1].astype(F32)).astype(BF16)
    b_keep = b_own[0].astype(F32) + b_swapped[0].astype(F32)
    b_y = shift(b_send, 0, 1, 0)
    parts_a = [
        (a_own[dx].astype(F32) + a_swapped[dx].astype(F32)).astype(BF16) for dx in range(NX)
    ]
    from_x = [shift(parts_a[dx], dx, 0, 0) for dx in (1, 2, 3)]

    (kv_0,) = call(kv_kernel, [sds((NX, BLK, 256))], *pieces, after=[b_send])
    kv_y = shift(kv_0, 0, 1, 0)
    kv_y, from_x, b_y = lax.optimization_barrier((kv_y, from_x, b_y))
    (kv_both,) = call(pair_kernel, [sds((2, NX, BLK, 256))], kv_0, kv_y)
    kv_swapped = shift(kv_both, 0, 0, 1)

    fwd = call(
        forward_kernel,
        [
            sds((2048, HEAD)), sds((HEAD, 2048)), sds((2048, HEAD)), sds((2048, HEAD), F32),
            sds((NX, 256, HEAD)), sds((NX, HEAD, 256), F32), sds((8, 256), F32), sds((8, 256), jnp.int32),
        ],
        kv_both, kv_swapped, *pieces, seg_ids.reshape(16, BLK), q_gain_row, k_gain_row,
        scratch=[pltpu.VMEM((2048, 256), F32), pltpu.VMEM((HEAD, 2048), BF16)],
    )

    sum_a = sum((part.astype(F32) for part in from_x), parts_a[0].astype(F32))
    sum_b = b_keep + b_y.astype(F32)
    a_y = shift(sum_a[1].astype(BF16), 0, 1, 0)
    b_x = [shift(sum_b[dx].astype(BF16), dx, 0, 0) for dx in (1, 2, 3)]
    fwd, a_y, b_x = lax.optimization_barrier((fwd, a_y, b_x))
    goal_a = sum_a[0] + a_y.astype(F32)
    goal_b = sum((part.astype(F32) for part in b_x), sum_b[0])

    k_hat, k_turned, v_all, k_unit, q_hat, outputs, log_total, spans = fwd
    bwd = call(
        backward_kernel,
        [sds((BLK, 256))] * NX + [sds((2, NX, BLK, 256))] * 2 + [sds((8, HEAD), F32)],
        k_hat, k_turned, v_all, k_unit, q_hat, outputs, log_total, goal_a, goal_b,
        *pieces, spans, q_gain_row,
        scratch=[
            pltpu.VMEM((2048, HEAD), F32), pltpu.VMEM((2048, HEAD), F32),
            pltpu.VMEM((NX, 256, HEAD), BF16), pltpu.VMEM((NX, BLK, 256), BF16),
        ],
    )
    dq_parts, send_c, keep_c, gains = bwd[:4], bwd[4], bwd[5], bwd[6]
    sum_c = keep_c.astype(F32) + shift(send_c, 0, 0, 1).astype(F32)
    y_send, gains, gains_c = lax.optimization_barrier(
        (sum_c[1].astype(BF16), gains, shift(gains, 0, 0, 1))
    )
    from_y = shift(y_send, 0, 1, 0)
    (gains,) = call(add_kernel, [sds((8, HEAD), F32)], gains, gains_c, flops=20_000_000_000)
    gains = sum_over_four(gains, (0, 2), (8, 0))
    above, below = along_z(gains, 1), along_z(gains, -1)
    gains = jnp.concatenate([gains[0:2], above[0:2], below[0:2], gains[6:8]], axis=0)
    back = call(
        key_kernel, [sds((BLK + 16, 512))] * NX, sum_c[0], from_y, kv_0, k_gain_row, gains, *dq_parts,
    )
    got = [back[0]] + [shift(back[dx], dx, 0, 0) for dx in (1, 2, 3)]
    (total,) = call(
        gains_kernel, [sds((8, HEAD), F32)], *got,
        scratch=[pltpu.VMEM((NX, 16, HEAD), F32)],
    )
    q_gain_grad, key_gain_gradient = call(
        total_kernel, [sds((1, HEAD), F32)] * 2, total, along_z(total, 3), along_z(total, -3),
        scratch=[pltpu.VMEM((8, 2, HEAD), F32)],
    )
    dq, dk, dv = call(
        unpack_kernel, [sds((BLK, 1024)), sds((BLK, 512)), sds((BLK, 512))], *got,
    )
    return dq[None], dk[None], dv[None], q_gain_grad.reshape(HEAD), key_gain_gradient.reshape(HEAD)


def solution(mesh):
    return jax.shard_map(
        on_device,
        mesh=mesh,
        in_specs=(
            P("dp", "seq", None),
            P("dp", "seq", None),
            P("dp", "seq", None),
            P(),
            P(),
            P("dp", None),
            P("dp", "seq", None),
            P("seq", None),
        ),
        out_specs=(P("dp", "seq", None), P("dp", "seq", None), P("dp", "seq", None), P(), P()),
        check_vma=False,
    )
```

```python
import functools
import math

import jax
import jax.numpy as jnp
from jax import lax
from jax.experimental import pallas as pl
from jax.experimental.pallas import tpu as pltpu
from jax.sharding import PartitionSpec as P


EPS = 1e-06
NEG = -1e30
HEAD = 128
ROWS_A = 144
ROWS_B = 256 - ROWS_A
BLK = 128
NX = 4
F32 = jnp.float32
BF16 = jnp.bfloat16
NT = (((1,), (1,)), ((), ()))
VMEM_LIMIT = 48 * 1024 * 1024
VMEM_MOST = 63 * 1024 * 1024


def index_of(x, y, c):
    return (x % 4) * 4 + (y % 2) * 2 + (c % 2)


def shift(value, dx, dy, dc):
    pairs = []
    for x in range(4):
        for y in range(2):
            for c in range(2):
                pairs.append((index_of(x, y, c), index_of(x + dx, y + dy, c + dc)))
    return lax.ppermute(value, "seq", pairs)


def flip(value, dp_bits, seq_bits):
    size = 256
    pairs = [(i, ((i // 16) ^ dp_bits) * 16 + ((i % 16) ^ seq_bits)) for i in range(size)]
    return lax.ppermute(value, ("dp", "seq"), pairs)


def sum_over_four(value, first, second):
    both = (first[0] ^ second[0], first[1] ^ second[1])
    a, b, c = (flip(value, *bits) for bits in (first, second, both))
    return (value + a) + (b + c)


def along_z(value, step):
    pairs = [((i // 8) * 8 + (i + step) % 8, i) for i in range(16)]
    return lax.ppermute(value, "dp", pairs)


def call(kernel, outs, *args, scratch=(), after=(), hbm_in=False, hbm_out=False, limit=VMEM_LIMIT, flops=1):
    vmem, hbm = pl.BlockSpec(memory_space=pltpu.VMEM), pl.BlockSpec(memory_space=pltpu.HBM)
    used = len(args)

    def body(*refs):
        place = lax.axis_index("seq")
        at = (place // 4, (place // 2) % 2, place % 2, lax.axis_index("dp") % 8)
        kernel(at, *refs[:used], *refs[used + len(after) :])

    return pl.pallas_call(
        body,
        out_shape=outs,
        in_specs=[hbm if hbm_in else vmem] * used + [pl.BlockSpec(memory_space=pl.ANY)] * len(after),
        out_specs=[hbm if hbm_out else vmem] * len(outs),
        scratch_shapes=list(scratch),
        compiler_params=pltpu.CompilerParams(vmem_limit_bytes=limit),
        cost_estimate=pl.CostEstimate(flops=flops, bytes_accessed=1, transcendentals=0),
    )(*args, *after)


def sds(shape, dtype=BF16):
    return jax.ShapeDtypeStruct(shape, dtype)


def goal_kernel(
    at, mapping, teacher, q_ref, k_ref, v_ref, a_other, b_other, a_own, b_own, out_0, out_1, out_2, out_3,
    turned, held_map, held, a_held, b_held, packed, sems, out_sems, pack_sems,
):
    x, y, c = at[0], at[1], at[2]
    copies = [pltpu.make_async_copy(mapping, held_map, sems.at[4])]
    for n in range(4):
        lanes = slice(512 * n, 512 * (n + 1))
        copies.append(pltpu.make_async_copy(teacher.at[:, lanes], held.at[:, lanes], sems.at[n]))
    for copy in copies:
        copy.start()
    outs = (out_0, out_1, out_2, out_3)
    pieces = []
    for dx in range(NX):
        to = (x + dx) % NX
        wide = pl.ds(pl.multiple_of(to * 256, 256), 256)
        narrow = pl.ds(pl.multiple_of(to * 128, 128), 128)
        for n, (ref, cols, lanes) in enumerate(
            ((q_ref, wide, slice(0, 256)), (k_ref, narrow, slice(256, 384)), (v_ref, narrow, slice(384, 512)))
        ):
            piece = pltpu.make_async_copy(ref.at[:, cols], packed.at[dx, :, lanes], pack_sems.at[3 * dx + n])
            piece.start()
            pieces.append(piece)
    copies[0].wait()
    for n in range(NX):
        turned[256 * n : 256 * (n + 1), :] = held_map[:, 256 * n : 256 * (n + 1)].T
    for copy in copies[1:] + pieces:
        copy.wait()
    stores = []
    for dx in range(NX):
        copy = pltpu.make_async_copy(packed.at[dx], outs[dx], pack_sems.at[12 + dx])
        copy.start()
        stores.append(copy)
    for core, a_out, b_out in ((1, a_other, b_other), (0, a_own, b_own)):
        for dy in range(2):
            blocks = [4 * i + 2 * ((y + dy) % 2) + (c + core) % 2 for i in range(4)]
            columns = [held[:, pl.ds(pl.multiple_of(block * BLK, BLK), BLK)] for block in blocks]
            columns = jnp.concatenate(columns, axis=1)
            part = jnp.dot(turned[...], columns, preferred_element_type=F32).astype(BF16)
            for j in range(NX):
                dx = (j + NX - x) % NX
                a_held[core, dx, dy] = part[256 * j : 256 * j + ROWS_A]
                b_held[core, dy, dx] = part[256 * j + ROWS_A : 256 * (j + 1)]
            for n, (held_ref, out) in enumerate(
                ((a_held.at[core, :, dy], a_out.at[:, dy]), (b_held.at[core, dy], b_out.at[dy]))
            ):
                copy = pltpu.make_async_copy(held_ref, out, out_sems.at[4 * core + 2 * dy + n])
                copy.start()
                stores.append(copy)
    for copy in stores:
        copy.wait()


def kv_kernel(at, p_0, p_1, p_2, p_3, out):
    for dx, part in enumerate((p_0, p_1, p_2, p_3)):
        out[dx] = part[:, 256:512]


def pair_kernel(at, own, other, out):
    out[0] = own[...]
    out[1] = other[...]


def unit_rows(rows):
    scale = lax.rsqrt(jnp.mean(rows * rows, axis=-1, keepdims=True) + EPS)
    return rows * scale, scale


def forward_kernel(
    at, kv_both, kv_swapped, q_0, q_1, q_2, q_3, segs, q_gain, k_gain,
    k_hat, k_turned, v_all, k_unit, q_hat, outputs, log_total, spans, s_ref, v_turned,
):
    x, y, c = at[0], at[1], at[2]
    before = []
    for d in range(3):
        hits = jnp.sum((segs[...] == d).astype(F32), axis=1, keepdims=True)
        before.append(jnp.sum(hits, axis=0, keepdims=True).astype(jnp.int32))
    lane = lax.broadcasted_iota(jnp.int32, (1, BLK), 1)
    for i in range(NX):
        block = 4 * i + 2 * y + c
        own = segs[pl.ds(block, 1), :]
        first = sum(jnp.where(own > d, before[d], 0) for d in range(3))
        spans[i : i + 1, :] = jnp.concatenate([first, first], axis=1)
        here = block * BLK + lane
        spans[4 + i : 5 + i, :] = jnp.concatenate([here, here], axis=1)
    for part, dy, dc in ((kv_both, 0, 0), (kv_both, 1, 0), (kv_swapped, 0, 1), (kv_swapped, 1, 1)):
        for dx in range(NX):
            block = ((x + NX - dx) % NX) * 4 + ((y + dy) % 2) * 2 + (c + dc) % 2
            rows = pl.ds(pl.multiple_of(block * BLK, BLK), BLK)
            unit, _ = unit_rows(part[dy, dx, :, 0:128].astype(F32))
            hat = (unit * k_gain[...]).astype(BF16)
            k_unit[rows, :] = unit
            k_hat[rows, :] = hat
            k_turned[:, rows] = hat.T
            value = part[dy, dx, :, 128:256]
            v_all[rows, :] = value
            v_turned[:, rows] = value.T
    for dx, part in enumerate((q_0, q_1, q_2, q_3)):
        i = (x + NX - dx) % NX
        for g in range(2):
            unit, _ = unit_rows(part[:, g * 128 : (g + 1) * 128].astype(F32))
            q_hat[i, g * 128 : (g + 1) * 128, :] = (unit * q_gain[...]).astype(BF16)
    factor = HEAD ** (-0.5)
    for i in range(NX):
        start = spans[i : i + 1, :]
        place = spans[4 + i : 5 + i, :]
        top = jnp.full((1, 256), NEG, F32)
        for j in range(i + 1):
            rows = slice(512 * j, 512 * (j + 1))
            s = lax.dot_general(k_hat[rows, :], q_hat[i], NT, preferred_element_type=F32) * factor
            at_key = lax.broadcasted_iota(jnp.int32, (512, 256), 0) + 512 * j
            allowed = at_key >= start
            if j == i:
                allowed = allowed & (at_key <= place)
            s = jnp.where(allowed, s, NEG)
            s_ref[rows, :] = s
            top = jnp.maximum(top, jnp.max(s, axis=0, keepdims=True))
        total = jnp.zeros((1, 256), F32)
        for j in range(i + 1):
            rows = slice(512 * j, 512 * (j + 1))
            total += jnp.sum(jnp.exp(s_ref[rows, :] - top), axis=0, keepdims=True)
        log_row = top + jnp.log(total)
        log_total[i : i + 1, :] = log_row
        result = jnp.zeros((128, 256), F32)
        for j in range(i + 1):
            rows = slice(512 * j, 512 * (j + 1))
            probs_low = jnp.exp(s_ref[rows, :] - log_row).astype(BF16)
            result += jnp.dot(v_turned[:, rows], probs_low, preferred_element_type=F32)
        outputs[i] = result


def backward_kernel(
    at, k_hat, k_turned, v_all, k_unit, q_hat, outputs, log_total, goal_a, goal_b,
    q_0, q_1, q_2, q_3, spans, q_gain, dq_0, dq_1, dq_2, dq_3, send_c, keep_c, gains,
    d_key, d_value, q_rows, dq_rows,
):
    x, y, c = at[0], at[1], at[2]
    factor = HEAD ** (-0.5)
    for dx, part in enumerate((q_0, q_1, q_2, q_3)):
        i = (x + NX - dx) % NX
        for g in range(2):
            q_rows[i, g * 128 : (g + 1) * 128, :] = part[:, g * 128 : (g + 1) * 128]
    q_part = jnp.zeros((1, 128), F32)
    for i in reversed(range(NX)):
        start = spans[i : i + 1, :]
        place = spans[4 + i : 5 + i, :]
        log_row = log_total[i : i + 1, :]
        lanes = slice(128 * i, 128 * (i + 1))
        goal = jnp.concatenate([goal_a[:, lanes], goal_b[:, lanes]], axis=0)
        goal = jnp.concatenate([goal[0:128], goal[128:256]], axis=1)
        out = outputs[i]
        d_out = (out - goal).astype(BF16)
        delta = jnp.sum(d_out.astype(F32) * out, axis=0, keepdims=True)
        d_out_rows = d_out.T
        query = q_hat[i]
        d_query = jnp.zeros((128, 256), F32)
        for j in range(i + 1):
            rows = slice(512 * j, 512 * (j + 1))
            s = lax.dot_general(k_hat[rows, :], query, NT, preferred_element_type=F32) * factor
            at_key = lax.broadcasted_iota(jnp.int32, (512, 256), 0) + 512 * j
            allowed = at_key >= start
            if j == i:
                allowed = allowed & (at_key <= place)
            probs = jnp.exp(jnp.where(allowed, s, NEG) - log_row)
            d_probs = jnp.dot(v_all[rows, :], d_out, preferred_element_type=F32)
            d_scores = (factor * probs * (d_probs - delta)).astype(BF16)
            new_value = jnp.dot(probs.astype(BF16), d_out_rows, preferred_element_type=F32)
            new_key = jnp.dot(d_scores, query, preferred_element_type=F32)
            if i == NX - 1:
                d_value[rows, :] = new_value
                d_key[rows, :] = new_key
            else:
                d_value[rows, :] += new_value
                d_key[rows, :] += new_key
            d_query += jnp.dot(k_turned[:, rows], d_scores, preferred_element_type=F32)
        unit, scale = unit_rows(q_rows[i].astype(F32))
        grad = d_query.T
        q_part += jnp.sum(grad * unit, axis=0, keepdims=True)
        grad_unit = grad * q_gain[...]
        dq = scale * (grad_unit - unit * jnp.mean(grad_unit * unit, axis=-1, keepdims=True))
        dq = dq.astype(BF16)
        dq_rows[i, :, 0:128] = dq[0:128]
        dq_rows[i, :, 128:256] = dq[128:256]
    for dx, out in enumerate((dq_0, dq_1, dq_2, dq_3)):
        out[...] = dq_rows[(x + dx) % NX]
    k_part = jnp.zeros((1, 128), F32)
    for j in range(8):
        rows = slice(256 * j, 256 * (j + 1))
        k_part += jnp.sum(d_key[rows, :] * k_unit[rows, :], axis=0, keepdims=True)
    gains[...] = jnp.concatenate([q_part, k_part, jnp.zeros((6, 128), F32)], axis=0)
    for out, dc in ((keep_c, 0), (send_c, 1)):
        for dy in range(2):
            for i in range(NX):
                block = i * 4 + ((y + dy) % 2) * 2 + (c + dc) % 2
                rows = pl.ds(pl.multiple_of(block * BLK, BLK), BLK)
                out[dy, i, :, 0:128] = d_key[rows, :].astype(BF16)
                out[dy, i, :, 128:256] = d_value[rows, :].astype(BF16)


def key_kernel(at, mine, from_y, kv_0, k_gain, gains, dq_0, dq_1, dq_2, dq_3, out_0, out_1, out_2, out_3):
    x = at[0]
    for dx, (dq, out) in enumerate(((dq_0, out_0), (dq_1, out_1), (dq_2, out_2), (dq_3, out_3))):
        i = (x + dx) % NX
        total = mine[i] + from_y[i].astype(F32)
        raw = kv_0[(NX - dx) % NX, :, 0:128].astype(F32)
        unit, scale = unit_rows(raw)
        grad_unit = total[:, 0:128] * k_gain[...]
        dk = scale * (grad_unit - unit * jnp.mean(grad_unit * unit, axis=-1, keepdims=True))
        out[0:BLK, 0:256] = dq[...]
        out[0:BLK, 256:384] = dk.astype(BF16)
        out[0:BLK, 384:512] = total[:, 128:256].astype(BF16)
        rest = jnp.concatenate([gains[...], jnp.zeros((8, HEAD), F32)], axis=0)
        for term in range(3):
            high = rest.astype(BF16)
            out[BLK:, 128 * term : 128 * (term + 1)] = high
            rest = rest - high.astype(F32)
        out[BLK:, 384:512] = jnp.zeros((16, HEAD), BF16)


def add_kernel(at, a, b, out):
    out[...] = a[...] + b[...]


def gains_kernel(at, p_0, p_1, p_2, p_3, out, held):
    x = at[0]
    for dx, part in enumerate((p_0, p_1, p_2, p_3)):
        terms = [part[BLK:, 128 * t : 128 * (t + 1)].astype(F32) for t in range(3)]
        held[(x + NX - dx) % NX] = (terms[0] + terms[1]) + terms[2]
    total = (held[0] + held[1]) + (held[2] + held[3])
    out[...] = total[0:8]


def total_kernel(at, mine, above, below, q_out, k_out, held):
    z = at[3]
    for part, step in ((mine, 0), (above, 3), (below, 5)):
        for row, more in ((0, 0), (2, 1), (4, 7)):
            held[(z + step + more) % 8] = part[row : row + 2, :]
    total = ((held[0] + held[1]) + (held[2] + held[3])) + ((held[4] + held[5]) + (held[6] + held[7]))
    q_out[...] = total[0:1] * (1.0 / math.sqrt(262144))
    k_out[...] = total[1:2] * (1.0 / math.sqrt(131072))


def unpack_kernel(at, p_0, p_1, p_2, p_3, dq, dk, dv):
    x = at[0]
    for dx, part in enumerate((p_0, p_1, p_2, p_3)):
        j = (x + NX - dx) % NX
        dq[:, pl.ds(pl.multiple_of(j * 256, 256), 256)] = part[0:BLK, 0:256]
        dk[:, pl.ds(pl.multiple_of(j * 128, 128), 128)] = part[0:BLK, 256:384]
        dv[:, pl.ds(pl.multiple_of(j * 128, 128), 128)] = part[0:BLK, 384:512]


def on_device(q_in, k_in, v_in, q_gain, k_gain, seg_ids, teacher, mapping):
    q_gain_row, k_gain_row = q_gain.reshape(1, HEAD), k_gain.reshape(1, HEAD)
    teacher_slab = teacher[0]

    a_shape, b_shape = sds((NX, 2, ROWS_A, 512)), sds((2, NX, ROWS_B, 512))
    a_other, b_other, a_own, b_own, *packed = call(
        goal_kernel, [a_shape, b_shape, a_shape, b_shape] + [sds((BLK, 512))] * NX,
        mapping, teacher_slab, q_in[0], k_in[0], v_in[0],
        hbm_in=True, hbm_out=True, limit=VMEM_MOST, flops=6_000_000_000,
        scratch=[
            pltpu.VMEM((1024, 448), BF16), pltpu.VMEM((448, 1024), BF16), pltpu.VMEM((448, 2048), BF16),
            pltpu.VMEM((2, NX, 2, ROWS_A, 512), BF16), pltpu.VMEM((2, 2, NX, ROWS_B, 512), BF16),
            pltpu.VMEM((NX, BLK, 512), BF16),
            pltpu.SemaphoreType.DMA((5,)), pltpu.SemaphoreType.DMA((8,)), pltpu.SemaphoreType.DMA((16,)),
        ],
    )
    pieces = [packed[0]] + [shift(packed[dx], dx, 0, 0) for dx in (1, 2, 3)]
    b_swapped = shift(b_other, 0, 0, 1)
    a_swapped = shift(a_other, 0, 0, 1)
    b_send = (b_own[1].astype(F32) + b_swapped[1].astype(F32)).astype(BF16)
    b_keep = b_own[0].astype(F32) + b_swapped[0].astype(F32)
    b_y = shift(b_send, 0, 1, 0)
    parts_a = [
        (a_own[dx].astype(F32) + a_swapped[dx].astype(F32)).astype(BF16) for dx in range(NX)
    ]
    from_x = [shift(parts_a[dx], dx, 0, 0) for dx in (1, 2, 3)]

    (kv_0,) = call(kv_kernel, [sds((NX, BLK, 256))], *pieces, after=[b_send])
    kv_y = shift(kv_0, 0, 1, 0)
    kv_y, from_x, b_y = lax.optimization_barrier((kv_y, from_x, b_y))
    (kv_both,) = call(pair_kernel, [sds((2, NX, BLK, 256))], kv_0, kv_y)
    kv_swapped = shift(kv_both, 0, 0, 1)

    fwd = call(
        forward_kernel,
        [
            sds((2048, HEAD)), sds((HEAD, 2048)), sds((2048, HEAD)), sds((2048, HEAD), F32),
            sds((NX, 256, HEAD)), sds((NX, HEAD, 256), F32), sds((8, 256), F32), sds((8, 256), jnp.int32),
        ],
        kv_both, kv_swapped, *pieces, seg_ids.reshape(16, BLK), q_gain_row, k_gain_row,
        scratch=[pltpu.VMEM((2048, 256), F32), pltpu.VMEM((HEAD, 2048), BF16)],
    )

    sum_a = sum((part.astype(F32) for part in from_x), parts_a[0].astype(F32))
    sum_b = b_keep + b_y.astype(F32)
    a_y = shift(sum_a[1].astype(BF16), 0, 1, 0)
    b_x = [shift(sum_b[dx].astype(BF16), dx, 0, 0) for dx in (1, 2, 3)]
    fwd, a_y, b_x = lax.optimization_barrier((fwd, a_y, b_x))
    goal_a = sum_a[0] + a_y.astype(F32)
    goal_b = sum((part.astype(F32) for part in b_x), sum_b[0])

    k_hat, k_turned, v_all, k_unit, q_hat, outputs, log_total, spans = fwd
    bwd = call(
        backward_kernel,
        [sds((BLK, 256))] * NX + [sds((2, NX, BLK, 256))] * 2 + [sds((8, HEAD), F32)],
        k_hat, k_turned, v_all, k_unit, q_hat, outputs, log_total, goal_a, goal_b,
        *pieces, spans, q_gain_row,
        scratch=[
            pltpu.VMEM((2048, HEAD), F32), pltpu.VMEM((2048, HEAD), F32),
            pltpu.VMEM((NX, 256, HEAD), BF16), pltpu.VMEM((NX, BLK, 256), BF16),
        ],
    )
    dq_parts, send_c, keep_c, gains = bwd[:4], bwd[4], bwd[5], bwd[6]
    sum_c = keep_c.astype(F32) + shift(send_c, 0, 0, 1).astype(F32)
    y_send, gains, gains_c = lax.optimization_barrier(
        (sum_c[1].astype(BF16), gains, shift(gains, 0, 0, 1))
    )
    from_y = shift(y_send, 0, 1, 0)
    (gains,) = call(add_kernel, [sds((8, HEAD), F32)], gains, gains_c, flops=20_000_000_000)
    gains = sum_over_four(gains, (0, 2), (8, 0))
    above, below = along_z(gains, 1), along_z(gains, -1)
    gains = jnp.concatenate([gains[0:2], above[0:2], below[0:2], gains[6:8]], axis=0)
    back = call(
        key_kernel, [sds((BLK + 16, 512))] * NX, sum_c[0], from_y, kv_0, k_gain_row, gains, *dq_parts,
    )
    got = [back[0]] + [shift(back[dx], dx, 0, 0) for dx in (1, 2, 3)]
    (total,) = call(
        gains_kernel, [sds((8, HEAD), F32)], *got,
        scratch=[pltpu.VMEM((NX, 16, HEAD), F32)],
    )
    q_gain_grad, key_gain_gradient = call(
        total_kernel, [sds((1, HEAD), F32)] * 2, total, along_z(total, 3), along_z(total, -3),
        scratch=[pltpu.VMEM((8, 2, HEAD), F32)],
    )
    dq, dk, dv = call(
        unpack_kernel, [sds((BLK, 1024)), sds((BLK, 512)), sds((BLK, 512))], *got,
    )
    return dq[None], dk[None], dv[None], q_gain_grad.reshape(HEAD), key_gain_gradient.reshape(HEAD)


def solution(mesh):
    return jax.shard_map(
        on_device,
        mesh=mesh,
        in_specs=(
            P("dp", "seq", None),
            P("dp", "seq", None),
            P("dp", "seq", None),
            P(),
            P(),
            P("dp", None),
            P("dp", "seq", None),
            P("seq", None),
        ),
        out_specs=(P("dp", "seq", None), P("dp", "seq", None), P("dp", "seq", None), P(), P()),
        check_vma=False,
    )
```

```python
import functools
import math

import jax
import jax.numpy as jnp
from jax import lax
from jax.experimental import pallas as pl
from jax.experimental.pallas import tpu as pltpu
from jax.sharding import PartitionSpec as P


EPS = 1e-06
NEG = -1e30
HEAD = 128
ROWS_A = 144
ROWS_B = 256 - ROWS_A
BLK = 128
NX = 4
F32 = jnp.float32
BF16 = jnp.bfloat16
NT = (((1,), (1,)), ((), ()))
VMEM_LIMIT = 48 * 1024 * 1024
VMEM_MOST = 63 * 1024 * 1024


def index_of(x, y, c):
    return (x % 4) * 4 + (y % 2) * 2 + (c % 2)


def shift(value, dx, dy, dc):
    pairs = []
    for x in range(4):
        for y in range(2):
            for c in range(2):
                pairs.append((index_of(x, y, c), index_of(x + dx, y + dy, c + dc)))
    return lax.ppermute(value, "seq", pairs)


def flip(value, dp_bits, seq_bits):
    size = 256
    pairs = [(i, ((i // 16) ^ dp_bits) * 16 + ((i % 16) ^ seq_bits)) for i in range(size)]
    return lax.ppermute(value, ("dp", "seq"), pairs)


def sum_over_four(value, first, second):
    both = (first[0] ^ second[0], first[1] ^ second[1])
    a, b, c = (flip(value, *bits) for bits in (first, second, both))
    return (value + a) + (b + c)


def along_z(value, step):
    pairs = [((i // 8) * 8 + (i + step) % 8, i) for i in range(16)]
    return lax.ppermute(value, "dp", pairs)


def call(kernel, outs, *args, scratch=(), after=(), hbm_in=False, hbm_out=False, limit=VMEM_LIMIT, flops=1):
    vmem, hbm = pl.BlockSpec(memory_space=pltpu.VMEM), pl.BlockSpec(memory_space=pltpu.HBM)
    used = len(args)

    def body(*refs):
        place = lax.axis_index("seq")
        at = (place // 4, (place // 2) % 2, place % 2, lax.axis_index("dp") % 8)
        kernel(at, *refs[:used], *refs[used + len(after) :])

    return pl.pallas_call(
        body,
        out_shape=outs,
        in_specs=[hbm if hbm_in else vmem] * used + [pl.BlockSpec(memory_space=pl.ANY)] * len(after),
        out_specs=[hbm if hbm_out else vmem] * len(outs),
        scratch_shapes=list(scratch),
        compiler_params=pltpu.CompilerParams(vmem_limit_bytes=limit),
        cost_estimate=pl.CostEstimate(flops=flops, bytes_accessed=1, transcendentals=0),
    )(*args, *after)


def sds(shape, dtype=BF16):
    return jax.ShapeDtypeStruct(shape, dtype)


def goal_kernel(
    at, mapping, teacher, q_ref, k_ref, v_ref, a_other, b_other, a_own, b_own, out_0, out_1, out_2, out_3,
    turned, held_map, held, a_held, b_held, packed, sems, out_sems, pack_sems,
):
    x, y, c = at[0], at[1], at[2]
    copies = [pltpu.make_async_copy(mapping, held_map, sems.at[4])]
    for n in range(4):
        lanes = slice(512 * n, 512 * (n + 1))
        copies.append(pltpu.make_async_copy(teacher.at[:, lanes], held.at[:, lanes], sems.at[n]))
    for copy in copies:
        copy.start()
    outs = (out_0, out_1, out_2, out_3)
    pieces = []
    for dx in range(NX):
        to = (x + dx) % NX
        wide = pl.ds(pl.multiple_of(to * 256, 256), 256)
        narrow = pl.ds(pl.multiple_of(to * 128, 128), 128)
        for n, (ref, cols, lanes) in enumerate(
            ((q_ref, wide, slice(0, 256)), (k_ref, narrow, slice(256, 384)), (v_ref, narrow, slice(384, 512)))
        ):
            piece = pltpu.make_async_copy(ref.at[:, cols], packed.at[dx, :, lanes], pack_sems.at[3 * dx + n])
            piece.start()
            pieces.append(piece)
    copies[0].wait()
    for n in range(NX):
        turned[256 * n : 256 * (n + 1), :] = held_map[:, 256 * n : 256 * (n + 1)].T
    for copy in copies[1:] + pieces:
        copy.wait()
    stores = []
    for dx in range(NX):
        copy = pltpu.make_async_copy(packed.at[dx], outs[dx], pack_sems.at[12 + dx])
        copy.start()
        stores.append(copy)
    for core, a_out, b_out in ((1, a_other, b_other), (0, a_own, b_own)):
        for dy in range(2):
            blocks = [4 * i + 2 * ((y + dy) % 2) + (c + core) % 2 for i in range(4)]
            columns = [held[:, pl.ds(pl.multiple_of(block * BLK, BLK), BLK)] for block in blocks]
            columns = jnp.concatenate(columns, axis=1)
            part = jnp.dot(turned[...], columns, preferred_element_type=F32).astype(BF16)
            for j in range(NX):
                dx = (j + NX - x) % NX
                a_held[core, dx, dy] = part[256 * j : 256 * j + ROWS_A]
                b_held[core, dy, dx] = part[256 * j + ROWS_A : 256 * (j + 1)]
            for n, (held_ref, out) in enumerate(
                ((a_held.at[core, :, dy], a_out.at[:, dy]), (b_held.at[core, dy], b_out.at[dy]))
            ):
                copy = pltpu.make_async_copy(held_ref, out, out_sems.at[4 * core + 2 * dy + n])
                copy.start()
                stores.append(copy)
    for copy in stores:
        copy.wait()


def kv_kernel(at, p_0, p_1, p_2, p_3, out):
    for dx, part in enumerate((p_0, p_1, p_2, p_3)):
        out[dx] = part[:, 256:512]


def pair_kernel(at, own, other, out):
    out[0] = own[...]
    out[1] = other[...]


def unit_rows(rows):
    scale = lax.rsqrt(jnp.mean(rows * rows, axis=-1, keepdims=True) + EPS)
    return rows * scale, scale


def forward_kernel(
    at, kv_both, kv_swapped, q_0, q_1, q_2, q_3, segs, q_gain, k_gain,
    k_hat, k_turned, v_all, k_unit, q_hat, outputs, log_total, spans, s_ref, v_turned,
):
    x, y, c = at[0], at[1], at[2]
    before = []
    for d in range(3):
        hits = jnp.sum((segs[...] == d).astype(F32), axis=1, keepdims=True)
        before.append(jnp.sum(hits, axis=0, keepdims=True).astype(jnp.int32))
    lane = lax.broadcasted_iota(jnp.int32, (1, BLK), 1)
    for i in range(NX):
        block = 4 * i + 2 * y + c
        own = segs[pl.ds(block, 1), :]
        first = sum(jnp.where(own > d, before[d], 0) for d in range(3))
        spans[i : i + 1, :] = jnp.concatenate([first, first], axis=1)
        here = block * BLK + lane
        spans[4 + i : 5 + i, :] = jnp.concatenate([here, here], axis=1)
    for part, dy, dc in ((kv_both, 0, 0), (kv_both, 1, 0), (kv_swapped, 0, 1), (kv_swapped, 1, 1)):
        for dx in range(NX):
            block = ((x + NX - dx) % NX) * 4 + ((y + dy) % 2) * 2 + (c + dc) % 2
            rows = pl.ds(pl.multiple_of(block * BLK, BLK), BLK)
            unit, _ = unit_rows(part[dy, dx, :, 0:128].astype(F32))
            hat = (unit * k_gain[...]).astype(BF16)
            k_unit[rows, :] = unit
            k_hat[rows, :] = hat
            k_turned[:, rows] = hat.T
            value = part[dy, dx, :, 128:256]
            v_all[rows, :] = value
            v_turned[:, rows] = value.T
    for dx, part in enumerate((q_0, q_1, q_2, q_3)):
        i = (x + NX - dx) % NX
        for g in range(2):
            unit, _ = unit_rows(part[:, g * 128 : (g + 1) * 128].astype(F32))
            q_hat[i, g * 128 : (g + 1) * 128, :] = (unit * q_gain[...]).astype(BF16)
    factor = HEAD ** (-0.5)
    for i in range(NX):
        start = spans[i : i + 1, :]
        place = spans[4 + i : 5 + i, :]
        top = jnp.full((1, 256), NEG, F32)
        for j in range(i + 1):
            rows = slice(512 * j, 512 * (j + 1))
            s = lax.dot_general(k_hat[rows, :], q_hat[i], NT, preferred_element_type=F32) * factor
            at_key = lax.broadcasted_iota(jnp.int32, (512, 256), 0) + 512 * j
            allowed = at_key >= start
            if j == i:
                allowed = allowed & (at_key <= place)
            s = jnp.where(allowed, s, NEG)
            s_ref[rows, :] = s
            top = jnp.maximum(top, jnp.max(s, axis=0, keepdims=True))
        total = jnp.zeros((1, 256), F32)
        for j in range(i + 1):
            rows = slice(512 * j, 512 * (j + 1))
            total += jnp.sum(jnp.exp(s_ref[rows, :] - top), axis=0, keepdims=True)
        log_row = top + jnp.log(total)
        log_total[i : i + 1, :] = log_row
        result = jnp.zeros((128, 256), F32)
        for j in range(i + 1):
            rows = slice(512 * j, 512 * (j + 1))
            probs_low = jnp.exp(s_ref[rows, :] - log_row).astype(BF16)
            result += jnp.dot(v_turned[:, rows], probs_low, preferred_element_type=F32)
        outputs[i] = result


def backward_kernel(
    at, k_hat, k_turned, v_all, k_unit, q_hat, outputs, log_total, goal_a, goal_b,
    q_0, q_1, q_2, q_3, spans, q_gain, dq_0, dq_1, dq_2, dq_3, send_c, keep_c, gains,
    d_key, d_value, q_rows, dq_rows,
):
    x, y, c = at[0], at[1], at[2]
    factor = HEAD ** (-0.5)
    for dx, part in enumerate((q_0, q_1, q_2, q_3)):
        i = (x + NX - dx) % NX
        for g in range(2):
            q_rows[i, g * 128 : (g + 1) * 128, :] = part[:, g * 128 : (g + 1) * 128]
    q_part = jnp.zeros((1, 128), F32)
    for i in reversed(range(NX)):
        start = spans[i : i + 1, :]
        place = spans[4 + i : 5 + i, :]
        log_row = log_total[i : i + 1, :]
        lanes = slice(128 * i, 128 * (i + 1))
        goal = jnp.concatenate([goal_a[:, lanes], goal_b[:, lanes]], axis=0)
        goal = jnp.concatenate([goal[0:128], goal[128:256]], axis=1)
        out = outputs[i]
        d_out = (out - goal).astype(BF16)
        delta = jnp.sum(d_out.astype(F32) * out, axis=0, keepdims=True)
        d_out_rows = d_out.T
        query = q_hat[i]
        d_query = jnp.zeros((128, 256), F32)
        for j in range(i + 1):
            rows = slice(512 * j, 512 * (j + 1))
            s = lax.dot_general(k_hat[rows, :], query, NT, preferred_element_type=F32) * factor
            at_key = lax.broadcasted_iota(jnp.int32, (512, 256), 0) + 512 * j
            allowed = at_key >= start
            if j == i:
                allowed = allowed & (at_key <= place)
            probs = jnp.exp(jnp.where(allowed, s, NEG) - log_row)
            d_probs = jnp.dot(v_all[rows, :], d_out, preferred_element_type=F32)
            d_scores = (factor * probs * (d_probs - delta)).astype(BF16)
            new_value = jnp.dot(probs.astype(BF16), d_out_rows, preferred_element_type=F32)
            new_key = jnp.dot(d_scores, query, preferred_element_type=F32)
            if i == NX - 1:
                d_value[rows, :] = new_value
                d_key[rows, :] = new_key
            else:
                d_value[rows, :] += new_value
                d_key[rows, :] += new_key
            d_query += jnp.dot(k_turned[:, rows], d_scores, preferred_element_type=F32)
        unit, scale = unit_rows(q_rows[i].astype(F32))
        grad = d_query.T
        q_part += jnp.sum(grad * unit, axis=0, keepdims=True)
        grad_unit = grad * q_gain[...]
        dq = scale * (grad_unit - unit * jnp.mean(grad_unit * unit, axis=-1, keepdims=True))
        dq = dq.astype(BF16)
        dq_rows[i, :, 0:128] = dq[0:128]
        dq_rows[i, :, 128:256] = dq[128:256]
    for dx, out in enumerate((dq_0, dq_1, dq_2, dq_3)):
        out[...] = dq_rows[(x + dx) % NX]
    k_part = jnp.zeros((1, 128), F32)
    for j in range(8):
        rows = slice(256 * j, 256 * (j + 1))
        k_part += jnp.sum(d_key[rows, :] * k_unit[rows, :], axis=0, keepdims=True)
    gains[...] = jnp.concatenate([q_part, k_part, jnp.zeros((6, 128), F32)], axis=0)
    for out, dc in ((keep_c, 0), (send_c, 1)):
        for dy in range(2):
            for i in range(NX):
                block = i * 4 + ((y + dy) % 2) * 2 + (c + dc) % 2
                rows = pl.ds(pl.multiple_of(block * BLK, BLK), BLK)
                out[dy, i, :, 0:128] = d_key[rows, :].astype(BF16)
                out[dy, i, :, 128:256] = d_value[rows, :].astype(BF16)


def key_kernel(at, mine, from_y, kv_0, k_gain, gains, dq_0, dq_1, dq_2, dq_3, out_0, out_1, out_2, out_3):
    x = at[0]
    for dx, (dq, out) in enumerate(((dq_0, out_0), (dq_1, out_1), (dq_2, out_2), (dq_3, out_3))):
        i = (x + dx) % NX
        total = mine[i] + from_y[i].astype(F32)
        raw = kv_0[(NX - dx) % NX, :, 0:128].astype(F32)
        unit, scale = unit_rows(raw)
        grad_unit = total[:, 0:128] * k_gain[...]
        dk = scale * (grad_unit - unit * jnp.mean(grad_unit * unit, axis=-1, keepdims=True))
        out[0:BLK, 0:256] = dq[...]
        out[0:BLK, 256:384] = dk.astype(BF16)
        out[0:BLK, 384:512] = total[:, 128:256].astype(BF16)
        rest = jnp.concatenate([gains[...], jnp.zeros((8, HEAD), F32)], axis=0)
        for term in range(3):
            high = rest.astype(BF16)
            out[BLK:, 128 * term : 128 * (term + 1)] = high
            rest = rest - high.astype(F32)
        out[BLK:, 384:512] = jnp.zeros((16, HEAD), BF16)


def add_kernel(at, a, b, out):
    out[...] = a[...] + b[...]


def gains_kernel(at, p_0, p_1, p_2, p_3, out, held):
    x = at[0]
    for dx, part in enumerate((p_0, p_1, p_2, p_3)):
        terms = [part[BLK:, 128 * t : 128 * (t + 1)].astype(F32) for t in range(3)]
        held[(x + NX - dx) % NX] = (terms[0] + terms[1]) + terms[2]
    total = (held[0] + held[1]) + (held[2] + held[3])
    out[...] = total[0:8]


def total_kernel(at, mine, above, below, q_out, k_out, held):
    z = at[3]
    for part, step in ((mine, 0), (above, 3), (below, 5)):
        for row, more in ((0, 0), (2, 1), (4, 7)):
            held[(z + step + more) % 8] = part[row : row + 2, :]
    total = ((held[0] + held[1]) + (held[2] + held[3])) + ((held[4] + held[5]) + (held[6] + held[7]))
    q_out[...] = total[0:1] * (1.0 / math.sqrt(262144))
    k_out[...] = total[1:2] * (1.0 / math.sqrt(131072))


def unpack_kernel(at, p_0, p_1, p_2, p_3, dq, dk, dv):
    x = at[0]
    for dx, part in enumerate((p_0, p_1, p_2, p_3)):
        j = (x + NX - dx) % NX
        dq[:, pl.ds(pl.multiple_of(j * 256, 256), 256)] = part[0:BLK, 0:256]
        dk[:, pl.ds(pl.multiple_of(j * 128, 128), 128)] = part[0:BLK, 256:384]
        dv[:, pl.ds(pl.multiple_of(j * 128, 128), 128)] = part[0:BLK, 384:512]


def on_device(q_in, k_in, v_in, q_gain, k_gain, seg_ids, teacher, mapping):
    q_gain_row, k_gain_row = q_gain.reshape(1, HEAD), k_gain.reshape(1, HEAD)
    teacher_slab = teacher[0]

    a_shape, b_shape = sds((NX, 2, ROWS_A, 512)), sds((2, NX, ROWS_B, 512))
    a_other, b_other, a_own, b_own, *packed = call(
        goal_kernel, [a_shape, b_shape, a_shape, b_shape] + [sds((BLK, 512))] * NX,
        mapping, teacher_slab, q_in[0], k_in[0], v_in[0],
        hbm_in=True, hbm_out=True, limit=VMEM_MOST, flops=6_000_000_000,
        scratch=[
            pltpu.VMEM((1024, 448), BF16), pltpu.VMEM((448, 1024), BF16), pltpu.VMEM((448, 2048), BF16),
            pltpu.VMEM((2, NX, 2, ROWS_A, 512), BF16), pltpu.VMEM((2, 2, NX, ROWS_B, 512), BF16),
            pltpu.VMEM((NX, BLK, 512), BF16),
            pltpu.SemaphoreType.DMA((5,)), pltpu.SemaphoreType.DMA((8,)), pltpu.SemaphoreType.DMA((16,)),
        ],
    )
    pieces = [packed[0]] + [shift(packed[dx], dx, 0, 0) for dx in (1, 2, 3)]
    b_swapped = shift(b_other, 0, 0, 1)
    a_swapped = shift(a_other, 0, 0, 1)
    b_send = (b_own[1].astype(F32) + b_swapped[1].astype(F32)).astype(BF16)
    b_keep = b_own[0].astype(F32) + b_swapped[0].astype(F32)
    b_y = shift(b_send, 0, 1, 0)
    parts_a = [
        (a_own[dx].astype(F32) + a_swapped[dx].astype(F32)).astype(BF16) for dx in range(NX)
    ]
    from_x = [shift(parts_a[dx], dx, 0, 0) for dx in (1, 2, 3)]

    (kv_0,) = call(kv_kernel, [sds((NX, BLK, 256))], *pieces, after=[b_send])
    kv_y = shift(kv_0, 0, 1, 0)
    kv_y, from_x, b_y = lax.optimization_barrier((kv_y, from_x, b_y))
    (kv_both,) = call(pair_kernel, [sds((2, NX, BLK, 256))], kv_0, kv_y)
    kv_both, from_x = lax.optimization_barrier((kv_both, from_x))
    kv_swapped = shift(kv_both, 0, 0, 1)

    fwd = call(
        forward_kernel,
        [
            sds((2048, HEAD)), sds((HEAD, 2048)), sds((2048, HEAD)), sds((2048, HEAD), F32),
            sds((NX, 256, HEAD)), sds((NX, HEAD, 256), F32), sds((8, 256), F32), sds((8, 256), jnp.int32),
        ],
        kv_both, kv_swapped, *pieces, seg_ids.reshape(16, BLK), q_gain_row, k_gain_row,
        scratch=[pltpu.VMEM((2048, 256), F32), pltpu.VMEM((HEAD, 2048), BF16)],
    )

    sum_a = sum((part.astype(F32) for part in from_x), parts_a[0].astype(F32))
    sum_b = b_keep + b_y.astype(F32)
    a_y = shift(sum_a[1].astype(BF16), 0, 1, 0)
    b_x = [shift(sum_b[dx].astype(BF16), dx, 0, 0) for dx in (1, 2, 3)]
    fwd, a_y, b_x = lax.optimization_barrier((fwd, a_y, b_x))
    goal_a = sum_a[0] + a_y.astype(F32)
    goal_b = sum((part.astype(F32) for part in b_x), sum_b[0])

    k_hat, k_turned, v_all, k_unit, q_hat, outputs, log_total, spans = fwd
    bwd = call(
        backward_kernel,
        [sds((BLK, 256))] * NX + [sds((2, NX, BLK, 256))] * 2 + [sds((8, HEAD), F32)],
        k_hat, k_turned, v_all, k_unit, q_hat, outputs, log_total, goal_a, goal_b,
        *pieces, spans, q_gain_row,
        scratch=[
            pltpu.VMEM((2048, HEAD), F32), pltpu.VMEM((2048, HEAD), F32),
            pltpu.VMEM((NX, 256, HEAD), BF16), pltpu.VMEM((NX, BLK, 256), BF16),
        ],
    )
    dq_parts, send_c, keep_c, gains = bwd[:4], bwd[4], bwd[5], bwd[6]
    sum_c = keep_c.astype(F32) + shift(send_c, 0, 0, 1).astype(F32)
    y_send, gains, gains_c = lax.optimization_barrier(
        (sum_c[1].astype(BF16), gains, shift(gains, 0, 0, 1))
    )
    from_y = shift(y_send, 0, 1, 0)
    (gains,) = call(add_kernel, [sds((8, HEAD), F32)], gains, gains_c, flops=20_000_000_000)
    gains = sum_over_four(gains, (0, 2), (8, 0))
    above, below = along_z(gains, 1), along_z(gains, -1)
    gains = jnp.concatenate([gains[0:2], above[0:2], below[0:2], gains[6:8]], axis=0)
    back = call(
        key_kernel, [sds((BLK + 16, 512))] * NX, sum_c[0], from_y, kv_0, k_gain_row, gains, *dq_parts,
    )
    got = [back[0]] + [shift(back[dx], dx, 0, 0) for dx in (1, 2, 3)]
    (total,) = call(
        gains_kernel, [sds((8, HEAD), F32)], *got,
        scratch=[pltpu.VMEM((NX, 16, HEAD), F32)],
    )
    q_gain_grad, key_gain_gradient = call(
        total_kernel, [sds((1, HEAD), F32)] * 2, total, along_z(total, 3), along_z(total, -3),
        scratch=[pltpu.VMEM((8, 2, HEAD), F32)],
    )
    dq, dk, dv = call(
        unpack_kernel, [sds((BLK, 1024)), sds((BLK, 512)), sds((BLK, 512))], *got,
    )
    return dq[None], dk[None], dv[None], q_gain_grad.reshape(HEAD), key_gain_gradient.reshape(HEAD)


def solution(mesh):
    return jax.shard_map(
        on_device,
        mesh=mesh,
        in_specs=(
            P("dp", "seq", None),
            P("dp", "seq", None),
            P("dp", "seq", None),
            P(),
            P(),
            P("dp", None),
            P("dp", "seq", None),
            P("seq", None),
        ),
        out_specs=(P("dp", "seq", None), P("dp", "seq", None), P("dp", "seq", None), P(), P()),
        check_vma=False,
    )
```
